32 devices in a mesh: gx: 4 (over x, core), gy: 8 (over z, y).
Axes of the slice: x: 2, y: 2, z: 4, core: 2. Of those that a mesh axis runs over, the one named last changes fastest.
Arguments:
- potential: float32 [64, 128, 256], P('gx', 'gy'), may hold values from -1 to 1
- charge: float32 [64, 128, 256], P('gx', 'gy'), may hold values from -6 to 6
- region: int32 [64, 128, 256], P('gx', 'gy'), may hold values from 0 to 16, as said below
- electrode_volts: float32 [16], replicated, may hold values from -2 to 2
Outputs:
- correction: float32 [64, 128, 256], P('gx', 'gy')
The draws below stay inside these ranges and needn't reach their ends.
Inputs may be any that keep to these rules, and one draw needn't show every extreme that they name: `region`: 0 marks a free cell; k marks a cell of electrode k, held at electrode_volts[k - 1]; about one cell in eight belongs to an electrode.
All inputs are finite; a program needn't handle non-finite values.
Results may differ from the reference program's by a relative error of at most 0.00002.
Values sent between devices are 32-bit elements; how exact they have to be, the bound alone decides.
A program may use at most 64 MiB of HBM per device.

```python
import jax
import jax.numpy as jnp

CZ = 256
LEVELS = 4
SWEEPS = 1
COARSE_SWEEPS = 4
REGIONS = 16
NX = 64
NY = 128


def draw_region(key, part):
    first_key, second_key = jax.random.split(key)
    picked = jax.random.randint(first_key, (NX, NY, CZ), 0, 8)
    electrode_ids = jax.random.randint(second_key, (NX, NY, CZ), 1, REGIONS + 1)
    return jnp.where(picked == 0, electrode_ids, 0).astype(jnp.int32)


def block_levels(own_key, dims, shards, low, largest):
    loudness, own = 1.0, jax.random.fold_in(own_key, 6)
    for axis_at, parts in shards:
        heights = jnp.exp(jax.random.uniform(jax.random.fold_in(own, axis_at), (parts,), jnp.float32, low / len(shards), largest / len(shards)))
        loudness = loudness * jnp.repeat(heights, dims[axis_at] // parts).reshape([-1 if axis == axis_at else 1 for axis in range(len(dims))])
    return loudness


def normal_values(stream_key, shape, deviation, reach, cuts=(), kind=jnp.bfloat16):
    entries = jax.random.normal(stream_key, shape, jnp.float32) * deviation
    if len(cuts) > 0:
        entries = block_levels(stream_key, shape, cuts, -0.22, 0.18) * entries
    return jnp.clip(entries, min=-reach, max=reach).astype(kind)


def setup_inputs(seed: int = 0) -> dict:
    keys = jax.random.split(jax.random.key(seed), 5)
    return {
        "potential": jnp.clip(jax.random.uniform(keys[0], (NX, NY, CZ), jnp.float32, -1.0, 1.0) * block_levels(keys[0], (NX, NY, CZ), ((0, 4), (1, 8)), -0.4, 0.0), -1.0, 1.0),
        "charge": normal_values(keys[1], (NX, NY, CZ), 1.0, 6.0, ((0, 4), (1, 8)), jnp.float32),
        "region": draw_region(jax.random.fold_in(keys[4], 71), 0),
        "electrode_volts": jnp.clip(jax.random.uniform(keys[3], (REGIONS,), jnp.float32, -2.0, 2.0), -2.0, 2.0),
    }


screen = 0.5


def pad_plane(values):
    return jnp.pad(values, ((1, 1), (1, 1), (0, 0)))


def neighbour_sums(padded):
    interior = padded[1:-1, 1:-1]
    flat_sum = padded[2:, 1:-1] + padded[:-2, 1:-1] + padded[1:-1, 2:] + padded[1:-1, :-2]
    padded_z = jnp.pad(interior, ((0, 0), (0, 0), (1, 1)))
    vertical = padded_z[:, :, 2:] + padded_z[:, :, :-2]
    return flat_sum, vertical


def checker(span_x, span_y, span_z):
    index_x = jnp.arange(span_x, dtype=jnp.int32)[:, None, None]
    index_y = jnp.arange(span_y, dtype=jnp.int32)[None, :, None]
    index_z = jnp.arange(span_z, dtype=jnp.int32)[None, None, :]
    return (index_x + index_y + index_z) % 2


def half_sweep(iterate, source, divisor, weight, movable, colour):
    flat_sum, vertical = neighbour_sums(pad_plane(iterate))
    renewed = (source + weight * flat_sum + vertical) / divisor
    span_x, span_y, span_z = iterate.shape
    update = checker(span_x, span_y, span_z) == colour
    if movable is not None:
        update = jnp.logical_and(update, movable)
    return jnp.where(update, renewed, iterate)


def full_sweep(iterate, source, divisor, weight, movable):
    iterate = half_sweep(iterate, source, divisor, weight, movable, 0)
    return half_sweep(iterate, source, divisor, weight, movable, 1)


def restrict(values):
    paired = values.reshape(values.shape[0] // 2, 2, values.shape[1], values.shape[2])
    even_rows, odd_rows = paired[:, 0], paired[:, 1]
    before = jnp.concatenate([jnp.zeros_like(odd_rows[:1]), odd_rows[:-1]], axis=0)
    across = 0.25 * before + 0.5 * even_rows + 0.25 * odd_rows
    paired = across.reshape(across.shape[0], across.shape[1] // 2, 2, across.shape[2])
    even_rows, odd_rows = paired[:, :, 0], paired[:, :, 1]
    before = jnp.concatenate([jnp.zeros_like(odd_rows[:, :1]), odd_rows[:, :-1]], axis=1)
    return 0.25 * before + 0.5 * even_rows + 0.25 * odd_rows


def coarsen(values):
    paired = values.reshape(values.shape[0] // 2, 2, values.shape[1], values.shape[2])
    across = 0.5 * (paired[:, 0] + paired[:, 1])
    paired = across.reshape(across.shape[0], across.shape[1] // 2, 2, across.shape[2])
    return 0.5 * (paired[:, :, 0] + paired[:, :, 1])


def solve_level(grid_level, source, coefficient, iterate, movable):
    weight = 0.25 ** grid_level
    divisor = (4.0 * weight + 2.0) + coefficient
    if grid_level == LEVELS - 1:
        for sweep_index in range(COARSE_SWEEPS):
            iterate = full_sweep(iterate, source, divisor, weight, None)
        return iterate
    for sweep_index in range(SWEEPS):
        iterate = full_sweep(iterate, source, divisor, weight, movable)
    flat_sum, vertical = neighbour_sums(pad_plane(iterate))
    residual = source - (divisor * iterate - (weight * flat_sum + vertical))
    if movable is not None:
        residual = jnp.where(movable, residual, 0.0)
    coarse_source = restrict(residual)
    coarse_coefficient = coarsen(coefficient)
    coarse = solve_level(grid_level + 1, coarse_source, coarse_coefficient, jnp.zeros_like(coarse_source), None)
    lifted = jnp.repeat(jnp.repeat(coarse, 2, axis=0), 2, axis=1)
    if movable is not None:
        lifted = jnp.where(movable, lifted, 0.0)
    iterate = iterate + lifted
    for sweep_index in range(SWEEPS):
        iterate = full_sweep(iterate, source, divisor, weight, movable)
    return iterate


def reference(potential, charge, region, electrode_volts):
    movable = region == 0
    dirichlet = jnp.zeros_like(potential)
    for electrode in range(REGIONS):
        dirichlet = dirichlet + jnp.where(region == electrode + 1, electrode_volts[electrode], jnp.float32(0.0))
    flat_sum, vertical = neighbour_sums(pad_plane(potential))
    source = charge - (6.0 * potential - (flat_sum + vertical)) - screen * (jnp.exp(potential) - 1.0)
    coefficient = screen * jnp.exp(potential)
    return solve_level(0, source, coefficient, dirichlet, movable)
```

```python
import functools

import jax
import jax.numpy as jnp
from jax import lax
from jax.experimental import pallas as pl
from jax.experimental.pallas import tpu as pltpu
from jax.sharding import PartitionSpec as P

MESH = pl.DeviceIdType.MESH
COARSE_SWEEPS = 4
REACH = 5

FACES = ((1, 0), (-1, 0), (0, 1), (0, -1))
AROUND = FACES + ((1, 1), (1, -1), (-1, 1), (-1, -1))
LOW_FACES = ((1, 0), (0, 1), (1, 1))
LOW_DEEP = FACES + ((1, 1), (1, -1), (-1, 1))


def cut(n, d, low, high):
    first, last = max(0, n * d - low), min(n, n * d + n + high)
    return first, first - n * d, last - first


def kernel(
    gx, gy, win_x, win_y,
    potential, charge, region, volts, out,
    pot, start, first, delta, reg, inv1, src1, inv2, src2, gat_i, gat_s, inv3, src3, e3, lift2, lift1, u0, u1, u2,
    send_sem, recv_sem, gsend_i, grecv_i, gsend_s, grecv_s,
):
    mx, my = lax.axis_index("gx"), lax.axis_index("gy")
    nx, ny, nz = out.shape
    used = [0]

    def here(dx, dy):
        x, y = mx + dx, my + dy
        ok = jnp.bool_(True)
        if dx:
            ok = jnp.logical_and(ok, jnp.logical_and(x >= 0, x < gx))
        if dy:
            ok = jnp.logical_and(ok, jnp.logical_and(y >= 0, y < gy))
        return ok, {"gx": x, "gy": y}

    def exchange(src, src_at, dst, dst_at, n, low, high, offsets):
        copies = []
        for dx, dy in offsets:
            fx, tx, cx = cut(n[0], dx, low, high)
            fy, ty, cy = cut(n[1], dy, low, high)
            ok, target = here(dx, dy)
            copy = pltpu.make_async_remote_copy(
                src_ref=src.at[pl.ds(src_at[0] + fx, cx), pl.ds(src_at[1] + fy, cy), :],
                dst_ref=dst.at[pl.ds(dst_at[0] + tx, cx), pl.ds(dst_at[1] + ty, cy), :],
                send_sem=send_sem.at[used[0]],
                recv_sem=recv_sem.at[used[0]],
                device_id=target,
                device_id_type=MESH,
            )
            used[0] += 1
            pl.when(ok)(copy.start)
            copies.append((ok, here(-dx, -dy)[0], copy))

        def wait():
            for sent, received, copy in copies:
                pl.when(received)(copy.wait_recv)
                pl.when(sent)(copy.wait_send)

        return wait

    def first_of(position, reach, span, total):
        return jnp.clip(position - reach, 0, total - span)

    base_x, base_y = first_of(mx, REACH, win_x, gx), first_of(my, REACH, win_y, gy)
    slot_x, slot_y = mx - base_x, my - base_y
    many_x = win_x if win_x == gx else 2 * win_x - 1
    many_y = win_y if win_y == gy else 2 * win_y - 1

    def partners(act):
        def one(index, carry):
            ix, iy = index // many_y, index % many_y
            tx = ix if win_x == gx else mx + ix - (win_x - 1)
            ty = iy if win_y == gy else my + iy - (win_y - 1)
            sends = (tx != mx) | (ty != my)
            takes = sends
            near_x, near_y, there_x, there_y = tx - base_x, ty - base_y, slot_x, slot_y
            if win_x != gx:
                there_x = mx - first_of(tx, REACH, win_x, gx)
                inside = (tx >= 0) & (tx < gx)
                sends = sends & inside & (there_x >= 0) & (there_x < win_x)
                takes = takes & inside & (near_x >= 0) & (near_x < win_x)
            if win_y != gy:
                there_y = my - first_of(ty, REACH, win_y, gy)
                inside = (ty >= 0) & (ty < gy)
                sends = sends & inside & (there_y >= 0) & (there_y < win_y)
                takes = takes & inside & (near_y >= 0) & (near_y < win_y)
            act((ix, iy), {"gx": tx, "gy": ty}, (near_x, near_y), (there_x, there_y), sends, takes)
            return carry + jnp.where(sends | takes, 1, 0)

        return lax.fori_loop(0, many_x * many_y, one, jnp.int32(0))

    def gather_copy(buffer, ssem, rsem, index, target, slot):
        return pltpu.make_async_remote_copy(
            src_ref=buffer.at[slot_x, slot_y],
            dst_ref=buffer.at[slot[0], slot[1]],
            send_sem=ssem.at[index[0], index[1]],
            recv_sem=rsem.at[slot[0], slot[1]],
            device_id=target,
            device_id_type=MESH,
        )

    def gather_start(buffer, ssem, rsem):
        def act(index, target, near, there, sends, takes):
            pl.when(sends)(gather_copy(buffer, ssem, rsem, index, target, there).start)

        partners(act)

    def gather_wait(buffer, ssem, rsem):
        def act(index, target, near, there, sends, takes):
            pl.when(takes)(gather_copy(buffer, ssem, rsem, index, target, near).wait_recv)
            pl.when(sends)(gather_copy(buffer, ssem, rsem, index, target, there).wait_send)

        partners(act)

    def parity(shape, offset):
        axes = [lax.broadcasted_iota(jnp.int32, shape, d) for d in range(3)]
        return (axes[0] + axes[1] + axes[2] + offset) & 1

    def vertical(v):
        k = lax.broadcasted_iota(jnp.int32, v.shape, 2)
        above = jnp.where(k == nz - 1, 0.0, pltpu.roll(v, nz - 1, 2))
        below = jnp.where(k == 0, 0.0, pltpu.roll(v, 1, 2))
        return above + below

    def flat(v):
        rows = v.shape[1]
        zero = jnp.zeros_like(v[:1])
        return (
            jnp.concatenate([v[1:], zero], axis=0)
            + jnp.concatenate([zero, v[:-1]], axis=0)
            + pltpu.roll(v, rows - 1, 1)
            + pltpu.roll(v, 1, 1)
        )

    def flat_of(ref, x, y, cx, cy):
        return (
            ref[x + 1 : x + 1 + cx, y : y + cy]
            + ref[x - 1 : x - 1 + cx, y : y + cy]
            + ref[x : x + cx, y + 1 : y + 1 + cy]
            + ref[x : x + cx, y - 1 : y - 1 + cy]
        )

    lanes = [(h, slice(128 * h, 128 * h + 128)) for h in range(nz // 128)]

    def put(buffer, i, rows, row):
        for h, lane in lanes:
            buffer[h, pl.ds(i, 1), rows] = row[None, :, lane]

    def every_other(buffer, count, y, rows):
        return jnp.concatenate(
            [buffer[h, :count, pl.ds(y, rows, stride=2)] for h, _ in lanes], axis=-1
        )

    def whole(buffer):
        return jnp.concatenate([buffer[h] for h, _ in lanes], axis=-1)

    def lift(buffer, i, y, row):
        for twice in range(2):
            for start_y in (y, y + 1):
                put(buffer, i + twice, pl.ds(start_y, row.shape[0], stride=2), row)

    for ref in (pot, start, first, delta, inv1, src1, inv2, src2, inv3, src3, e3, lift1, lift2):
        ref[...] = jnp.zeros(ref.shape, ref.dtype)
    reg[...] = jnp.ones(reg.shape, reg.dtype)

    barrier = pltpu.get_barrier_semaphore()

    def greet(index, target, near, there, sends, takes):
        @pl.when(sends | takes)
        def _():
            pl.semaphore_signal(barrier, inc=1, device_id=target, device_id_type=MESH)

    peers = partners(greet)
    if win_x == gx and win_y == gy:
        peers = gx * gy - 1

    p = potential[...]
    ids = region[...]
    movable = ids == 0
    dirichlet = jnp.zeros(p.shape, jnp.float32)
    for electrode in range(volts.shape[0]):
        dirichlet = jnp.where(ids == electrode + 1, volts[electrode], dirichlet)
    start[1 : nx + 1, 8 : ny + 8] = dirichlet
    pot[1 : nx + 1, 8 : ny + 8] = p
    reg[1 : nx + 1, 8 : ny + 8] = ids

    pl.semaphore_wait(barrier, peers)

    full = (nx, ny)
    wait_pot = exchange(potential, (0, 0), pot, (1, 8), full, 1, 1, FACES)
    wait_start = exchange(start, (1, 8), start, (1, 8), full, 1, 1, FACES)
    wait_reg = exchange(region, (0, 0), reg, (1, 8), full, 1, 0, LOW_FACES)

    bend = 0.5 * jnp.exp(p)
    inverse = 1.0 / (6.0 + bend)

    def coarsened(values, buffer):
        half_x, rows = values.shape[0] // 2, values.shape[1] // 2
        for i in range(half_x):
            put(buffer, i, slice(0, 2 * rows), 0.5 * (values[2 * i] + values[2 * i + 1]))
        return 0.5 * (every_other(buffer, half_x, 0, rows) + every_other(buffer, half_x, 1, rows))

    n1, n2, n3 = (nx // 2, ny // 2), (nx // 4, ny // 4), (nx // 8, ny // 8)
    c1 = coarsened(bend, u0)
    inv1[3 : 3 + n1[0], 8 : 8 + n1[1]] = 1.0 / (3.0 + c1)
    c2 = coarsened(c1, u1)
    inv2[4 : 4 + n2[0], 4 : 4 + n2[1]] = 1.0 / (2.25 + c2)
    c3 = coarsened(c2, u2)
    gat_i[pl.ds(slot_x, 1), pl.ds(slot_y, 1)] = (1.0 / (2.0625 + c3))[None, None]

    wait_pot()
    source = (
        charge[...]
        - (6.0 * p - (flat_of(pot, 1, 8, nx, ny) + vertical(p)))
        - (bend - 0.5)
    )
    wait_start()
    color = parity((nx, ny, nz), 0)
    even = jnp.logical_and(movable, color == 0)
    odd = jnp.logical_and(movable, color == 1)

    e = start[1 : nx + 1, 8 : ny + 8]
    e = jnp.where(even, (source + flat_of(start, 1, 8, nx, ny) + vertical(e)) * inverse, e)
    first[1 : nx + 1, 8 : ny + 8] = e
    wait_e = exchange(first, (1, 8), first, (1, 8), full, 1, 1, FACES)
    wait_inv1 = exchange(inv1, (3, 8), inv1, (3, 8), n1, 3, 3, AROUND)
    wait_inv2 = exchange(inv2, (4, 4), inv2, (4, 4), n2, 4, 4, AROUND)
    gather_start(gat_i, gsend_i, grecv_i)
    up_down = vertical(e)
    wait_e()
    new = (source + flat_of(first, 1, 8, nx, ny) + up_down) * inverse
    delta[2 : nx + 2, 8 : ny + 8] = jnp.where(odd, new, 0.0)
    wait_delta = exchange(delta, (2, 8), delta, (2, 8), full, 2, 1, LOW_DEEP)
    wait_reg()
    wait_inv1()
    wait_inv2()
    wait_delta()

    def narrowed(r, x, y, count, rows, buffer):
        width = r.shape[1]
        for i in range(count):
            a = x + 2 * i
            put(buffer, i, slice(0, width), 0.25 * r[a] + 0.5 * r[a + 1] + 0.25 * r[a + 2])
        return (
            0.25 * every_other(buffer, count, y, rows)
            + 0.5 * every_other(buffer, count, y + 1, rows)
            + 0.25 * every_other(buffer, count, y + 2, rows)
        )

    r = flat_of(delta, 1, 7, nx + 1, ny + 1) + vertical(delta[1 : nx + 2, 7 : ny + 8])
    live = jnp.logical_and(reg[:, 7 : ny + 8] == 0, parity(r.shape, 0) == 0)
    r = jnp.where(live, r, 0.0)
    src1[3 : 3 + n1[0], 8 : 8 + n1[1]] = narrowed(r, 0, 0, n1[0], n1[1], u0)
    wait_src1 = exchange(src1, (3, 8), src1, (3, 8), n1, 3, 3, AROUND)
    wait_src1()

    def down(src, inv, weight, offset):
        inverse, source = inv[...], src[...]
        color = parity(inv.shape, offset)
        red = jnp.where(color == 0, source * inverse, 0.0)
        black = jnp.where(color == 1, (source + weight * flat(red) + vertical(red)) * inverse, 0.0)
        r = jnp.where(
            jnp.logical_and(color == 0, inverse > 0.0), weight * flat(black) + vertical(black), 0.0
        )
        return red + black, r

    def sweep(e, source, inverse, weight, color):
        for c in range(2):
            e = jnp.where(color == c, (source + weight * flat(e) + vertical(e)) * inverse, e)
        return e

    e1, r = down(src1, inv1, 0.25, 1)
    src2[4 : 4 + n2[0], 4 : 4 + n2[1]] = narrowed(r, 2, 7, n2[0], n2[1], u1)
    wait_src2 = exchange(src2, (4, 4), src2, (4, 4), n2, 4, 4, AROUND)
    gather_wait(gat_i, gsend_i, grecv_i)
    for ix in range(win_x):
        for iy in range(win_y):
            inv3[2 * ix : 2 * ix + 2, 8 + 2 * iy : 10 + 2 * iy] = gat_i[ix, iy]
    wait_src2()
    e2, r = down(src2, inv2, 0.0625, 0)
    gat_s[pl.ds(slot_x, 1), pl.ds(slot_y, 1)] = narrowed(r, 3, 3, n3[0], n3[1], u2)[None, None]
    gather_start(gat_s, gsend_s, grecv_s)
    gather_wait(gat_s, gsend_s, grecv_s)
    for ix in range(win_x):
        for iy in range(win_y):
            src3[2 * ix : 2 * ix + 2, 8 + 2 * iy : 10 + 2 * iy] = gat_s[ix, iy]

    span3 = 2 * win_x
    color = parity(inv3.shape, 0)
    e3[2 : 2 + span3] = jnp.where(color == 0, src3[...] * inv3[...], 0.0)
    e = e3[2 : 2 + span3]
    e = jnp.where(
        color == 1, (src3[...] + 0.015625 * flat(e) + vertical(e)) * inv3[...], e
    )
    e3[2 : 2 + span3] = e

    def again(index, carry):
        e3[2 : 2 + span3] = sweep(e3[2 : 2 + span3], src3[...], inv3[...], 0.015625, parity(inv3.shape, 0))
        return carry

    lax.fori_loop(1, COARSE_SWEEPS, again, 0)

    for i in range(n3[0] + 4):
        row = e3[pl.ds(2 * slot_x + i, 1)]
        row = pltpu.roll(row, e3.shape[1] - 2 * slot_y, 1)[0, 6 : 10 + n3[1]]
        lift(lift2, 2 * i, 0, row)
    e2 = sweep(e2 + whole(lift2), src2[...], inv2[...], 0.0625, parity(inv2.shape, 0))
    for i in range(n2[0] + 2):
        lift(lift1, 1 + 2 * i, 6, e2[3 + i, 3 : 5 + n2[1]])
    e1 = sweep(e1 + whole(lift1), src1[...], inv1[...], 0.25, parity(inv1.shape, 1))
    for i in range(n1[0]):
        lift(u0, 2 * i, 0, e1[3 + i, 8 : 8 + n1[1]])
    e = first[1 : nx + 1, 8 : ny + 8] + delta[2 : nx + 2, 8 : ny + 8]
    e = e + jnp.where(movable, whole(u0)[:, :ny], 0.0)
    for buffer, chosen in ((start, even), (pot, odd)):
        buffer[1 : nx + 1, 8 : ny + 8] = e
        wait_up = exchange(buffer, (1, 8), buffer, (1, 8), full, 1, 1, FACES)
        up_down = vertical(e)
        wait_up()
        e = jnp.where(chosen, (source + flat_of(buffer, 1, 8, nx, ny) + up_down) * inverse, e)
    out[...] = e


def solution(mesh):
    gx, gy = mesh.shape["gx"], mesh.shape["gy"]
    win_x, win_y = min(gx, 2 * REACH + 1), min(gy, 2 * REACH + 1)
    many_x = win_x if win_x == gx else 2 * win_x - 1
    many_y = win_y if win_y == gy else 2 * win_y - 1

    def body(potential, charge, region, volts):
        nx, ny, nz = potential.shape
        f32 = jnp.float32

        def room(x, y, kind=f32):
            return pltpu.VMEM((x, y, nz), kind)

        def halves(x, y):
            return pltpu.VMEM((nz // 128, x, y, 128), f32)

        rows3 = -(-(2 * win_y + 16) // 8) * 8
        scratch = [
            room(nx + 2, ny + 16),
            room(nx + 2, ny + 16),
            room(nx + 2, ny + 16),
            room(nx + 3, ny + 16),
            room(nx + 1, ny + 8, jnp.int32),
            room(nx // 2 + 6, ny // 2 + 16),
            room(nx // 2 + 6, ny // 2 + 16),
            room(nx // 4 + 8, ny // 4 + 12),
            room(nx // 4 + 8, ny // 4 + 12),
            pltpu.VMEM((win_x, win_y, nx // 8, ny // 8, nz), f32),
            pltpu.VMEM((win_x, win_y, nx // 8, ny // 8, nz), f32),
            room(2 * win_x, rows3),
            room(2 * win_x, rows3),
            room(2 * win_x + 4, rows3),
            halves(nx // 4 + 8, ny // 4 + 12),
            halves(nx // 2 + 6, ny // 2 + 16),
            halves(nx, ny + 8),
            halves(nx // 2, ny // 2 + 16),
            halves(nx // 4, ny // 4 + 12),
            pltpu.SemaphoreType.DMA((64,)),
            pltpu.SemaphoreType.DMA((64,)),
            pltpu.SemaphoreType.DMA((many_x, many_y)),
            pltpu.SemaphoreType.DMA((win_x, win_y)),
            pltpu.SemaphoreType.DMA((many_x, many_y)),
            pltpu.SemaphoreType.DMA((win_x, win_y)),
        ]
        return pl.pallas_call(
            functools.partial(kernel, gx, gy, win_x, win_y),
            out_shape=jax.ShapeDtypeStruct(potential.shape, f32),
            in_specs=[pl.BlockSpec(memory_space=pltpu.VMEM)] * 3 + [pl.BlockSpec(memory_space=pltpu.SMEM)],
            out_specs=pl.BlockSpec(memory_space=pltpu.VMEM),
            scratch_shapes=scratch,
            compiler_params=pltpu.CompilerParams(
                collective_id=0, has_side_effects=True, vmem_limit_bytes=48 * 1024 * 1024
            ),
        )(potential, charge, region, volts)

    placed = (P("gx", "gy", None), P("gx", "gy", None), P("gx", "gy", None), P())
    return jax.shard_map(
        body, mesh=mesh, in_specs=placed, out_specs=P("gx", "gy", None), check_vma=False
    )
```

```python
import functools

import jax
import jax.numpy as jnp
from jax import lax
from jax.experimental import pallas as pl
from jax.experimental.pallas import tpu as pltpu
from jax.sharding import PartitionSpec as P

MESH = pl.DeviceIdType.MESH
COARSE_SWEEPS = 4
REACH = 5

FACES = ((1, 0), (-1, 0), (0, 1), (0, -1))
AROUND = FACES + ((1, 1), (1, -1), (-1, 1), (-1, -1))
LOW_FACES = ((1, 0), (0, 1), (1, 1))
LOW_DEEP = FACES + ((1, 1), (1, -1), (-1, 1))


def cut(n, d, low, high):
    first, last = max(0, n * d - low), min(n, n * d + n + high)
    return first, first - n * d, last - first


def kernel(
    gx, gy, win_x, win_y,
    potential, charge, region, volts, out,
    pot, start, first, delta, reg, inv1, src1, inv2, src2, gat_i, gat_s, inv3, src3, e3, lift2, lift1, u0, u1, u2,
    send_sem, recv_sem, gsend_i, grecv_i, gsend_s, grecv_s, charges, volt, in_sem,
):
    mx, my = lax.axis_index("gx"), lax.axis_index("gy")
    nx, ny, nz = out.shape
    used = [0]

    def here(dx, dy):
        x, y = mx + dx, my + dy
        ok = jnp.bool_(True)
        if dx:
            ok = jnp.logical_and(ok, jnp.logical_and(x >= 0, x < gx))
        if dy:
            ok = jnp.logical_and(ok, jnp.logical_and(y >= 0, y < gy))
        return ok, {"gx": x, "gy": y}

    def exchange(src, src_at, dst, dst_at, n, low, high, offsets):
        copies = []
        for dx, dy in offsets:
            fx, tx, cx = cut(n[0], dx, low, high)
            fy, ty, cy = cut(n[1], dy, low, high)
            ok, target = here(dx, dy)
            copy = pltpu.make_async_remote_copy(
                src_ref=src.at[pl.ds(src_at[0] + fx, cx), pl.ds(src_at[1] + fy, cy), :],
                dst_ref=dst.at[pl.ds(dst_at[0] + tx, cx), pl.ds(dst_at[1] + ty, cy), :],
                send_sem=send_sem.at[used[0]],
                recv_sem=recv_sem.at[used[0]],
                device_id=target,
                device_id_type=MESH,
            )
            used[0] += 1
            pl.when(ok)(copy.start)
            copies.append((ok, here(-dx, -dy)[0], copy))

        def wait():
            for sent, received, copy in copies:
                pl.when(received)(copy.wait_recv)
                pl.when(sent)(copy.wait_send)

        return wait

    def first_of(position, reach, span, total):
        return jnp.clip(position - reach, 0, total - span)

    base_x, base_y = first_of(mx, REACH, win_x, gx), first_of(my, REACH, win_y, gy)
    slot_x, slot_y = mx - base_x, my - base_y
    many_x = win_x if win_x == gx else 2 * win_x - 1
    many_y = win_y if win_y == gy else 2 * win_y - 1

    def partners(act):
        def one(index, carry):
            ix, iy = index // many_y, index % many_y
            tx = ix if win_x == gx else mx + ix - (win_x - 1)
            ty = iy if win_y == gy else my + iy - (win_y - 1)
            sends = (tx != mx) | (ty != my)
            takes = sends
            near_x, near_y, there_x, there_y = tx - base_x, ty - base_y, slot_x, slot_y
            if win_x != gx:
                there_x = mx - first_of(tx, REACH, win_x, gx)
                inside = (tx >= 0) & (tx < gx)
                sends = sends & inside & (there_x >= 0) & (there_x < win_x)
                takes = takes & inside & (near_x >= 0) & (near_x < win_x)
            if win_y != gy:
                there_y = my - first_of(ty, REACH, win_y, gy)
                inside = (ty >= 0) & (ty < gy)
                sends = sends & inside & (there_y >= 0) & (there_y < win_y)
                takes = takes & inside & (near_y >= 0) & (near_y < win_y)
            act((ix, iy), {"gx": tx, "gy": ty}, (near_x, near_y), (there_x, there_y), sends, takes)
            return carry + jnp.where(sends | takes, 1, 0)

        if many_x * many_y > 64:
            return lax.fori_loop(0, many_x * many_y, one, jnp.int32(0))
        for index in range(many_x * many_y):
            one(index, 0)
        return None

    def gather_copy(buffer, ssem, rsem, index, target, slot):
        return pltpu.make_async_remote_copy(
            src_ref=buffer.at[slot_x, slot_y],
            dst_ref=buffer.at[slot[0], slot[1]],
            send_sem=ssem.at[index[0], index[1]],
            recv_sem=rsem.at[slot[0], slot[1]],
            device_id=target,
            device_id_type=MESH,
        )

    def gather_start(buffer, ssem, rsem):
        def act(index, target, near, there, sends, takes):
            pl.when(sends)(gather_copy(buffer, ssem, rsem, index, target, there).start)

        partners(act)

    def gather_wait(buffer, ssem, rsem):
        def act(index, target, near, there, sends, takes):
            pl.when(takes)(gather_copy(buffer, ssem, rsem, index, target, near).wait_recv)
            pl.when(sends)(gather_copy(buffer, ssem, rsem, index, target, there).wait_send)

        partners(act)

    def parity(shape, offset):
        axes = [lax.broadcasted_iota(jnp.int32, shape, d) for d in range(3)]
        return (axes[0] + axes[1] + axes[2] + offset) & 1

    def vertical(v):
        k = lax.broadcasted_iota(jnp.int32, v.shape, 2)
        above = jnp.where(k == nz - 1, 0.0, pltpu.roll(v, nz - 1, 2))
        below = jnp.where(k == 0, 0.0, pltpu.roll(v, 1, 2))
        return above + below

    def flat(v):
        rows = v.shape[1]
        zero = jnp.zeros_like(v[:1])
        return (
            jnp.concatenate([v[1:], zero], axis=0)
            + jnp.concatenate([zero, v[:-1]], axis=0)
            + pltpu.roll(v, rows - 1, 1)
            + pltpu.roll(v, 1, 1)
        )

    def flat_of(ref, x, y, cx, cy):
        return (
            ref[x + 1 : x + 1 + cx, y : y + cy]
            + ref[x - 1 : x - 1 + cx, y : y + cy]
            + ref[x : x + cx, y + 1 : y + 1 + cy]
            + ref[x : x + cx, y - 1 : y - 1 + cy]
        )

    lanes = [(h, slice(128 * h, 128 * h + 128)) for h in range(nz // 128)]

    def put(buffer, i, rows, row):
        for h, lane in lanes:
            buffer[h, pl.ds(i, 1), rows] = row[None, :, lane]

    def every_other(buffer, count, y, rows):
        return jnp.concatenate(
            [buffer[h, :count, pl.ds(y, rows, stride=2)] for h, _ in lanes], axis=-1
        )

    def whole(buffer):
        return jnp.concatenate([buffer[h] for h, _ in lanes], axis=-1)

    def lift(buffer, i, y, row):
        for twice in range(2):
            for start_y in (y, y + 1):
                put(buffer, i + twice, pl.ds(start_y, row.shape[0], stride=2), row)

    pot[...] = jnp.zeros(pot.shape, jnp.float32)
    reg[...] = jnp.ones(reg.shape, jnp.int32)
    loads = [
        pltpu.make_async_copy(source, target, in_sem.at[index])
        for index, (source, target) in enumerate(
            (
                (region, reg.at[1 : nx + 1, 8 : ny + 8]),
                (potential, pot.at[1 : nx + 1, 8 : ny + 8]),
                (charge, charges),
                (volts, volt),
            )
        )
    ]
    for load in loads:
        load.start()
    for ref in (start, first, delta, inv1, src1, inv2, src2, inv3, src3, e3, lift1, lift2):
        ref[...] = jnp.zeros(ref.shape, ref.dtype)

    barrier = pltpu.get_barrier_semaphore()

    def greet(index, target, near, there, sends, takes):
        @pl.when(sends | takes)
        def _():
            pl.semaphore_signal(barrier, inc=1, device_id=target, device_id_type=MESH)

    peers = partners(greet)
    if win_x == gx and win_y == gy:
        peers = gx * gy - 1

    for load in loads:
        load.wait()
    p = pot[1 : nx + 1, 8 : ny + 8]
    ids = reg[1 : nx + 1, 8 : ny + 8]
    movable = ids == 0
    dirichlet = jnp.zeros(p.shape, jnp.float32)
    for electrode in range(volts.shape[0]):
        dirichlet = jnp.where(ids == electrode + 1, volt[electrode], dirichlet)
    start[1 : nx + 1, 8 : ny + 8] = dirichlet

    pl.semaphore_wait(barrier, peers)

    full = (nx, ny)
    wait_pot = exchange(pot, (1, 8), pot, (1, 8), full, 1, 1, FACES)
    wait_start = exchange(start, (1, 8), start, (1, 8), full, 1, 1, FACES)
    wait_reg = exchange(reg, (1, 8), reg, (1, 8), full, 1, 0, LOW_FACES)

    bend = 0.5 * jnp.exp(p)
    inverse = 1.0 / (6.0 + bend)

    def coarsened(values, buffer):
        half_x, rows = values.shape[0] // 2, values.shape[1] // 2
        for i in range(half_x):
            put(buffer, i, slice(0, 2 * rows), 0.5 * (values[2 * i] + values[2 * i + 1]))
        return 0.5 * (every_other(buffer, half_x, 0, rows) + every_other(buffer, half_x, 1, rows))

    n1, n2, n3 = (nx // 2, ny // 2), (nx // 4, ny // 4), (nx // 8, ny // 8)
    c1 = coarsened(bend, u0)
    inv1[3 : 3 + n1[0], 8 : 8 + n1[1]] = 1.0 / (3.0 + c1)
    c2 = coarsened(c1, u1)
    inv2[4 : 4 + n2[0], 4 : 4 + n2[1]] = 1.0 / (2.25 + c2)
    c3 = coarsened(c2, u2)
    gat_i[pl.ds(slot_x, 1), pl.ds(slot_y, 1)] = (1.0 / (2.0625 + c3))[None, None]

    wait_pot()
    source = (
        charges[...]
        - (6.0 * p - (flat_of(pot, 1, 8, nx, ny) + vertical(p)))
        - (bend - 0.5)
    )
    wait_start()
    color = parity((nx, ny, nz), 0)
    even = jnp.logical_and(movable, color == 0)
    odd = jnp.logical_and(movable, color == 1)

    e = start[1 : nx + 1, 8 : ny + 8]
    e = jnp.where(even, (source + flat_of(start, 1, 8, nx, ny) + vertical(e)) * inverse, e)
    first[1 : nx + 1, 8 : ny + 8] = e
    wait_e = exchange(first, (1, 8), first, (1, 8), full, 1, 1, FACES)
    wait_inv1 = exchange(inv1, (3, 8), inv1, (3, 8), n1, 3, 3, AROUND)
    wait_inv2 = exchange(inv2, (4, 4), inv2, (4, 4), n2, 4, 4, AROUND)
    gather_start(gat_i, gsend_i, grecv_i)
    up_down = vertical(e)
    wait_e()
    new = (source + flat_of(first, 1, 8, nx, ny) + up_down) * inverse
    delta[2 : nx + 2, 8 : ny + 8] = jnp.where(odd, new, 0.0)
    wait_delta = exchange(delta, (2, 8), delta, (2, 8), full, 2, 1, LOW_DEEP)
    wait_reg()
    wait_inv1()
    wait_inv2()
    wait_delta()

    def narrowed(r, x, y, count, rows, buffer):
        width = r.shape[1]
        for i in range(count):
            a = x + 2 * i
            put(buffer, i, slice(0, width), 0.25 * r[a] + 0.5 * r[a + 1] + 0.25 * r[a + 2])
        return (
            0.25 * every_other(buffer, count, y, rows)
            + 0.5 * every_other(buffer, count, y + 1, rows)
            + 0.25 * every_other(buffer, count, y + 2, rows)
        )

    r = flat_of(delta, 1, 7, nx + 1, ny + 1) + vertical(delta[1 : nx + 2, 7 : ny + 8])
    live = jnp.logical_and(reg[:, 7 : ny + 8] == 0, parity(r.shape, 0) == 0)
    r = jnp.where(live, r, 0.0)
    src1[3 : 3 + n1[0], 8 : 8 + n1[1]] = narrowed(r, 0, 0, n1[0], n1[1], u0)
    wait_src1 = exchange(src1, (3, 8), src1, (3, 8), n1, 3, 3, AROUND)
    wait_src1()

    def down(src, inv, weight, offset):
        inverse, source = inv[...], src[...]
        color = parity(inv.shape, offset)
        red = jnp.where(color == 0, source * inverse, 0.0)
        black = jnp.where(color == 1, (source + weight * flat(red) + vertical(red)) * inverse, 0.0)
        r = jnp.where(
            jnp.logical_and(color == 0, inverse > 0.0), weight * flat(black) + vertical(black), 0.0
        )
        return red + black, r

    def sweep(e, source, inverse, weight, color):
        for c in range(2):
            e = jnp.where(color == c, (source + weight * flat(e) + vertical(e)) * inverse, e)
        return e

    e1, r = down(src1, inv1, 0.25, 1)
    src2[4 : 4 + n2[0], 4 : 4 + n2[1]] = narrowed(r, 2, 7, n2[0], n2[1], u1)
    wait_src2 = exchange(src2, (4, 4), src2, (4, 4), n2, 4, 4, AROUND)
    gather_wait(gat_i, gsend_i, grecv_i)
    for ix in range(win_x):
        for iy in range(win_y):
            inv3[2 * ix : 2 * ix + 2, 8 + 2 * iy : 10 + 2 * iy] = gat_i[ix, iy]
    wait_src2()
    e2, r = down(src2, inv2, 0.0625, 0)
    gat_s[pl.ds(slot_x, 1), pl.ds(slot_y, 1)] = narrowed(r, 3, 3, n3[0], n3[1], u2)[None, None]
    gather_start(gat_s, gsend_s, grecv_s)
    gather_wait(gat_s, gsend_s, grecv_s)
    for ix in range(win_x):
        for iy in range(win_y):
            src3[2 * ix : 2 * ix + 2, 8 + 2 * iy : 10 + 2 * iy] = gat_s[ix, iy]

    span3 = 2 * win_x
    color = parity(inv3.shape, 0)
    e3[2 : 2 + span3] = jnp.where(color == 0, src3[...] * inv3[...], 0.0)
    e = e3[2 : 2 + span3]
    e = jnp.where(
        color == 1, (src3[...] + 0.015625 * flat(e) + vertical(e)) * inv3[...], e
    )
    e3[2 : 2 + span3] = e

    def again(index, carry):
        e3[2 : 2 + span3] = sweep(e3[2 : 2 + span3], src3[...], inv3[...], 0.015625, parity(inv3.shape, 0))
        return carry

    lax.fori_loop(1, COARSE_SWEEPS, again, 0)

    for i in range(n3[0] + 4):
        row = e3[pl.ds(2 * slot_x + i, 1)]
        row = pltpu.roll(row, e3.shape[1] - 2 * slot_y, 1)[0, 6 : 10 + n3[1]]
        lift(lift2, 2 * i, 0, row)
    e2 = sweep(e2 + whole(lift2), src2[...], inv2[...], 0.0625, parity(inv2.shape, 0))
    for i in range(n2[0] + 2):
        lift(lift1, 1 + 2 * i, 6, e2[3 + i, 3 : 5 + n2[1]])
    e1 = sweep(e1 + whole(lift1), src1[...], inv1[...], 0.25, parity(inv1.shape, 1))
    for i in range(n1[0]):
        lift(u0, 2 * i, 0, e1[3 + i, 8 : 8 + n1[1]])
    e = first[1 : nx + 1, 8 : ny + 8] + delta[2 : nx + 2, 8 : ny + 8]
    e = e + jnp.where(movable, whole(u0)[:, :ny], 0.0)
    for buffer, chosen in ((start, even), (pot, odd)):
        buffer[1 : nx + 1, 8 : ny + 8] = e
        wait_up = exchange(buffer, (1, 8), buffer, (1, 8), full, 1, 1, FACES)
        up_down = vertical(e)
        wait_up()
        e = jnp.where(chosen, (source + flat_of(buffer, 1, 8, nx, ny) + up_down) * inverse, e)
    out[...] = e


def solution(mesh):
    gx, gy = mesh.shape["gx"], mesh.shape["gy"]
    win_x, win_y = min(gx, 2 * REACH + 1), min(gy, 2 * REACH + 1)
    many_x = win_x if win_x == gx else 2 * win_x - 1
    many_y = win_y if win_y == gy else 2 * win_y - 1

    def body(potential, charge, region, volts):
        nx, ny, nz = potential.shape
        f32 = jnp.float32

        def room(x, y, kind=f32):
            return pltpu.VMEM((x, y, nz), kind)

        def halves(x, y):
            return pltpu.VMEM((nz // 128, x, y, 128), f32)

        rows3 = -(-(2 * win_y + 16) // 8) * 8
        scratch = [
            room(nx + 2, ny + 16),
            room(nx + 2, ny + 16),
            room(nx + 2, ny + 16),
            room(nx + 3, ny + 16),
            room(nx + 1, ny + 8, jnp.int32),
            room(nx // 2 + 6, ny // 2 + 16),
            room(nx // 2 + 6, ny // 2 + 16),
            room(nx // 4 + 8, ny // 4 + 12),
            room(nx // 4 + 8, ny // 4 + 12),
            pltpu.VMEM((win_x, win_y, nx // 8, ny // 8, nz), f32),
            pltpu.VMEM((win_x, win_y, nx // 8, ny // 8, nz), f32),
            room(2 * win_x, rows3),
            room(2 * win_x, rows3),
            room(2 * win_x + 4, rows3),
            halves(nx // 4 + 8, ny // 4 + 12),
            halves(nx // 2 + 6, ny // 2 + 16),
            halves(nx, ny + 8),
            halves(nx // 2, ny // 2 + 16),
            halves(nx // 4, ny // 4 + 12),
            pltpu.SemaphoreType.DMA((64,)),
            pltpu.SemaphoreType.DMA((64,)),
            pltpu.SemaphoreType.DMA((many_x, many_y)),
            pltpu.SemaphoreType.DMA((win_x, win_y)),
            pltpu.SemaphoreType.DMA((many_x, many_y)),
            pltpu.SemaphoreType.DMA((win_x, win_y)),
            room(nx, ny),
            pltpu.SMEM(volts.shape, f32),
            pltpu.SemaphoreType.DMA((4,)),
        ]
        return pl.pallas_call(
            functools.partial(kernel, gx, gy, win_x, win_y),
            out_shape=jax.ShapeDtypeStruct(potential.shape, f32),
            in_specs=[pl.BlockSpec(memory_space=pl.ANY)] * 4,
            out_specs=pl.BlockSpec(memory_space=pltpu.VMEM),
            scratch_shapes=scratch,
            compiler_params=pltpu.CompilerParams(
                collective_id=0, has_side_effects=True, vmem_limit_bytes=60 * 1024 * 1024
            ),
        )(potential, charge, region, volts)

    placed = (P("gx", "gy", None), P("gx", "gy", None), P("gx", "gy", None), P())
    return jax.shard_map(
        body, mesh=mesh, in_specs=placed, out_specs=P("gx", "gy", None), check_vma=False
    )
```

```python
import functools

import jax
import jax.numpy as jnp
from jax import lax
from jax.experimental import pallas as pl
from jax.experimental.pallas import tpu as pltpu
from jax.sharding import PartitionSpec as P

MESH = pl.DeviceIdType.MESH
COARSE_SWEEPS = 4
REACH = 5

FACES = ((1, 0), (-1, 0), (0, 1), (0, -1))
AROUND = FACES + ((1, 1), (1, -1), (-1, 1), (-1, -1))
NEAR = tuple((x, y) for x in range(-2, 3) for y in range(-2, 3) if x or y)
FREE = 1e30


def cut(n, d, low, high):
    first, last = max(0, n * d - low), min(n, n * d + n + high)
    return first, first - n * d, last - first


def kernel(
    gx, gy, win_x, win_y,
    potential, charge, region, volts, out,
    pot, code, chg, delta, start, first, source_rim, inverse_rim, ids, inv1, src1, inv2, src2, gat_i, gat_s, inv3, src3, e3, lift2, lift1, u0, u1, u2,
    send_sem, recv_sem, gsend_i, grecv_i, gsend_s, grecv_s, volt, in_sem,
):
    mx, my = lax.axis_index("gx"), lax.axis_index("gy")
    nx, ny, nz = out.shape
    used = [0]

    def here(dx, dy):
        x, y = mx + dx, my + dy
        ok = jnp.bool_(True)
        if dx:
            ok = jnp.logical_and(ok, jnp.logical_and(x >= 0, x < gx))
        if dy:
            ok = jnp.logical_and(ok, jnp.logical_and(y >= 0, y < gy))
        return ok, {"gx": x, "gy": y}

    def exchange(src, src_at, dst, dst_at, n, low, high, offsets):
        copies = []
        for dx, dy in offsets:
            fx, tx, cx = cut(n[0], dx, low, high)
            fy, ty, cy = cut(n[1], dy, low, high)
            ok, target = here(dx, dy)
            copy = pltpu.make_async_remote_copy(
                src_ref=src.at[pl.ds(src_at[0] + fx, cx), pl.ds(src_at[1] + fy, cy), :],
                dst_ref=dst.at[pl.ds(dst_at[0] + tx, cx), pl.ds((dst_at[1] + ty) % dst.shape[1], cy), :],
                send_sem=send_sem.at[used[0]],
                recv_sem=recv_sem.at[used[0]],
                device_id=target,
                device_id_type=MESH,
            )
            used[0] += 1
            pl.when(ok)(copy.start)
            copies.append((ok, here(-dx, -dy)[0], copy))

        def wait():
            for sent, received, copy in copies:
                pl.when(received)(copy.wait_recv)
                pl.when(sent)(copy.wait_send)

        return wait

    def first_of(position, reach, span, total):
        return jnp.clip(position - reach, 0, total - span)

    base_x, base_y = first_of(mx, REACH, win_x, gx), first_of(my, REACH, win_y, gy)
    slot_x, slot_y = mx - base_x, my - base_y
    many_x = win_x if win_x == gx else 2 * win_x - 1
    many_y = win_y if win_y == gy else 2 * win_y - 1

    def partners(act):
        def one(index, carry):
            ix, iy = index // many_y, index % many_y
            tx = ix if win_x == gx else mx + ix - (win_x - 1)
            ty = iy if win_y == gy else my + iy - (win_y - 1)
            sends = (tx != mx) | (ty != my)
            takes = sends
            near_x, near_y, there_x, there_y = tx - base_x, ty - base_y, slot_x, slot_y
            if win_x != gx:
                there_x = mx - first_of(tx, REACH, win_x, gx)
                inside = (tx >= 0) & (tx < gx)
                sends = sends & inside & (there_x >= 0) & (there_x < win_x)
                takes = takes & inside & (near_x >= 0) & (near_x < win_x)
            if win_y != gy:
                there_y = my - first_of(ty, REACH, win_y, gy)
                inside = (ty >= 0) & (ty < gy)
                sends = sends & inside & (there_y >= 0) & (there_y < win_y)
                takes = takes & inside & (near_y >= 0) & (near_y < win_y)
            act((ix, iy), {"gx": tx, "gy": ty}, (near_x, near_y), (there_x, there_y), sends, takes)
            return carry + jnp.where(sends | takes, 1, 0)

        if many_x * many_y > 64:
            return lax.fori_loop(0, many_x * many_y, one, jnp.int32(0))
        for index in range(many_x * many_y):
            one(index, 0)
        return None

    def gather_copy(buffer, ssem, rsem, index, target, slot):
        return pltpu.make_async_remote_copy(
            src_ref=buffer.at[slot_x, slot_y],
            dst_ref=buffer.at[slot[0], slot[1]],
            send_sem=ssem.at[index[0], index[1]],
            recv_sem=rsem.at[slot[0], slot[1]],
            device_id=target,
            device_id_type=MESH,
        )

    def gather_start(buffer, ssem, rsem):
        def act(index, target, near, there, sends, takes):
            pl.when(sends)(gather_copy(buffer, ssem, rsem, index, target, there).start)

        partners(act)

    def gather_wait(buffer, ssem, rsem):
        def act(index, target, near, there, sends, takes):
            pl.when(takes)(gather_copy(buffer, ssem, rsem, index, target, near).wait_recv)
            pl.when(sends)(gather_copy(buffer, ssem, rsem, index, target, there).wait_send)

        partners(act)

    def parity(shape, offset):
        axes = [lax.broadcasted_iota(jnp.int32, shape, d) for d in range(3)]
        return (axes[0] + axes[1] + axes[2] + offset) & 1

    def vertical(v):
        k = lax.broadcasted_iota(jnp.int32, v.shape, 2)
        above = jnp.where(k == nz - 1, 0.0, pltpu.roll(v, nz - 1, 2))
        below = jnp.where(k == 0, 0.0, pltpu.roll(v, 1, 2))
        return above + below

    def flat(v):
        rows = v.shape[1]
        zero = jnp.zeros_like(v[:1])
        return (
            jnp.concatenate([v[1:], zero], axis=0)
            + jnp.concatenate([zero, v[:-1]], axis=0)
            + pltpu.roll(v, rows - 1, 1)
            + pltpu.roll(v, 1, 1)
        )

    def flat_of(ref, x, y, cx, cy):
        return (
            ref[x + 1 : x + 1 + cx, y : y + cy]
            + ref[x - 1 : x - 1 + cx, y : y + cy]
            + ref[x : x + cx, y + 1 : y + 1 + cy]
            + ref[x : x + cx, y - 1 : y - 1 + cy]
        )

    lanes = [(h, slice(128 * h, 128 * h + 128)) for h in range(nz // 128)]

    def put(buffer, i, rows, row):
        for h, lane in lanes:
            buffer[h, pl.ds(i, 1), rows] = row[None, :, lane]

    def every_other(buffer, count, y, rows):
        return jnp.concatenate(
            [buffer[h, :count, pl.ds(y, rows, stride=2)] for h, _ in lanes], axis=-1
        )

    def whole(buffer):
        return jnp.concatenate([buffer[h] for h, _ in lanes], axis=-1)

    def lift(buffer, i, y, row):
        for twice in range(2):
            for start_y in (y, y + 1):
                put(buffer, i + twice, pl.ds(start_y, row.shape[0], stride=2), row)

    for ref in (pot, chg):
        ref[...] = jnp.zeros(ref.shape, jnp.float32)
    own = (slice(2, nx + 2), slice(8, ny + 8))
    rim = (slice(1, nx + 3), slice(7, ny + 9))
    loads = [
        pltpu.make_async_copy(source, target, in_sem.at[index])
        for index, (source, target) in enumerate(
            (
                (volts, volt),
                (region, ids),
                (potential, pot.at[own[0], own[1]]),
                (charge, chg.at[own[0], own[1]]),
            )
        )
    ]
    for load in loads:
        load.start()
    for ref in (code, delta, inv1, src1, inv2, src2, inv3, src3, e3, lift1, lift2):
        ref[...] = jnp.zeros(ref.shape, ref.dtype)

    barrier = pltpu.get_barrier_semaphore()

    def greet(index, target, near, there, sends, takes):
        @pl.when(sends | takes)
        def _():
            pl.semaphore_signal(barrier, inc=1, device_id=target, device_id_type=MESH)

    peers = partners(greet)
    if win_x == gx and win_y == gy:
        peers = gx * gy - 1

    for load in loads:
        load.wait()
    coded = jnp.full((nx, ny, nz), FREE, jnp.float32)
    for electrode in range(volts.shape[0]):
        coded = jnp.where(ids[...] == electrode + 1, volt[electrode], coded)
    code[own] = coded

    pl.semaphore_wait(barrier, peers)

    full = (nx, ny)
    wait_code = exchange(code, (2, 8), code, (2, 8), full, 2, 2, AROUND)
    wait_pot = exchange(pot, (2, 8), pot, (2, 8), full, 2, 2, AROUND)
    wait_chg = exchange(chg, (2, 8), chg, (2, 8), full, 1, 1, AROUND)

    bend = 0.5 * jnp.exp(pot[own])

    def coarsened(values, buffer):
        half_x, rows = values.shape[0] // 2, values.shape[1] // 2
        for i in range(half_x):
            put(buffer, i, slice(0, 2 * rows), 0.5 * (values[2 * i] + values[2 * i + 1]))
        return 0.5 * (every_other(buffer, half_x, 0, rows) + every_other(buffer, half_x, 1, rows))

    n1, n2, n3 = (nx // 2, ny // 2), (nx // 4, ny // 4), (nx // 8, ny // 8)
    c1 = coarsened(bend, u0)
    inv1[4 : 4 + n1[0], 8 : 8 + n1[1]] = 1.0 / (3.0 + c1)
    c2 = coarsened(c1, u1)
    inv2[5 : 5 + n2[0], 4 : 4 + n2[1]] = 1.0 / (2.25 + c2)
    c3 = coarsened(c2, u2)
    gat_i[pl.ds(slot_x, 1), pl.ds(slot_y, 1)] = (1.0 / (2.0625 + c3))[None, None]

    wait_code()
    wait_pot()
    wait_chg()
    wait_inv1 = exchange(inv1, (4, 8), inv1, (4, 8), n1, 4, 4, AROUND)
    wait_inv2 = exchange(inv2, (5, 4), inv2, (5, 4), n2, 5, 5, NEAR)
    gather_start(gat_i, gsend_i, grecv_i)
    coded = code[...]
    start[...] = jnp.where(coded == FREE, 0.0, coded)

    p = pot[rim]
    bend = 0.5 * jnp.exp(p)
    inverse = 1.0 / (6.0 + bend)
    source = (
        chg[rim]
        - (6.0 * p - (flat_of(pot, 1, 7, nx + 2, ny + 2) + vertical(p)))
        - (bend - 0.5)
    )
    movable = code[rim] == FREE
    color = parity(p.shape, 0)
    even = jnp.logical_and(movable, color == 0)
    e = start[rim]
    e = jnp.where(even, (source + flat_of(start, 1, 7, nx + 2, ny + 2) + vertical(e)) * inverse, e)
    first[rim] = e
    inverse_rim[...] = inverse
    source_rim[...] = source
    inner = (slice(1, nx + 1), slice(1, ny + 1))

    def odd_half(buffer):
        return (
            source_rim[inner] + flat_of(buffer, 2, 8, nx, ny) + vertical(buffer[own])
        ) * inverse_rim[inner]

    odd = jnp.logical_and(code[own] == FREE, parity((nx, ny, nz), 0) == 1)
    delta[own] = jnp.where(odd, odd_half(first), 0.0)
    wait_delta = exchange(delta, (2, 8), delta, (2, 8), full, 2, 2, AROUND)
    wait_inv1()
    wait_inv2()
    wait_delta()

    def narrowed(r, x, y, count, rows, buffer):
        width = r.shape[1]
        for i in range(count):
            a = x + 2 * i
            put(buffer, i, slice(0, width), 0.25 * r[a] + 0.5 * r[a + 1] + 0.25 * r[a + 2])
        return (
            0.25 * every_other(buffer, count, y, rows)
            + 0.5 * every_other(buffer, count, y + 1, rows)
            + 0.25 * every_other(buffer, count, y + 2, rows)
        )

    r = flat_of(delta, 1, 7, nx + 1, ny + 1) + vertical(delta[1 : nx + 2, 7 : ny + 8])
    live = jnp.logical_and(code[1 : nx + 2, 7 : ny + 8] == FREE, parity(r.shape, 0) == 0)
    r = jnp.where(live, r, 0.0)
    src1[4 : 4 + n1[0], 8 : 8 + n1[1]] = narrowed(r, 0, 0, n1[0], n1[1], u0)
    wait_src1 = exchange(src1, (4, 8), src1, (4, 8), n1, 4, 4, AROUND)
    wait_src1()

    def down(src, inv, weight, offset):
        inverse, source = inv[...], src[...]
        color = parity(inv.shape, offset)
        red = jnp.where(color == 0, source * inverse, 0.0)
        black = jnp.where(color == 1, (source + weight * flat(red) + vertical(red)) * inverse, 0.0)
        r = jnp.where(
            jnp.logical_and(color == 0, inverse > 0.0), weight * flat(black) + vertical(black), 0.0
        )
        return black, r

    def sweep(e, source, inverse, weight, color):
        for c in range(2):
            e = jnp.where(color == c, (source + weight * flat(e) + vertical(e)) * inverse, e)
        return e

    e1, r = down(src1, inv1, 0.25, 0)
    src2[5 : 5 + n2[0], 4 : 4 + n2[1]] = narrowed(r, 3, 7, n2[0], n2[1], u1)
    wait_src2 = exchange(src2, (5, 4), src2, (5, 4), n2, 5, 5, NEAR)
    gather_wait(gat_i, gsend_i, grecv_i)
    for ix in range(win_x):
        for iy in range(win_y):
            inv3[2 * ix : 2 * ix + 2, 8 + 2 * iy : 10 + 2 * iy] = gat_i[ix, iy]
    wait_src2()
    e2, r = down(src2, inv2, 0.0625, 1)
    gat_s[pl.ds(slot_x, 1), pl.ds(slot_y, 1)] = narrowed(r, 4, 3, n3[0], n3[1], u2)[None, None]
    gather_start(gat_s, gsend_s, grecv_s)
    gather_wait(gat_s, gsend_s, grecv_s)
    for ix in range(win_x):
        for iy in range(win_y):
            src3[2 * ix : 2 * ix + 2, 8 + 2 * iy : 10 + 2 * iy] = gat_s[ix, iy]

    span3 = 2 * win_x
    color = parity(inv3.shape, 0)
    e3[2 : 2 + span3] = jnp.where(color == 0, src3[...] * inv3[...], 0.0)
    e = e3[2 : 2 + span3]
    e = jnp.where(
        color == 1, (src3[...] + 0.015625 * flat(e) + vertical(e)) * inv3[...], e
    )
    e3[2 : 2 + span3] = e

    def again(index, carry):
        e3[2 : 2 + span3] = sweep(e3[2 : 2 + span3], src3[...], inv3[...], 0.015625, parity(inv3.shape, 0))
        return carry

    lax.fori_loop(1, COARSE_SWEEPS, again, 0)

    for i in range(n3[0] + 4):
        row = e3[pl.ds(2 * slot_x + i, 1)]
        row = pltpu.roll(row, e3.shape[1] - 2 * slot_y, 1)[0, 6 : 10 + n3[1]]
        lift(lift2, 1 + 2 * i, 0, row)
    e2 = sweep(e2 + whole(lift2), src2[...], inv2[...], 0.0625, parity(inv2.shape, 1))
    for i in range(n2[0] + 4):
        lift(lift1, 2 * i, 4, e2[3 + i, 2 : 6 + n2[1]])
    e1 = sweep(e1 + whole(lift1), src1[...], inv1[...], 0.25, parity(inv1.shape, 0))
    for i in range(n1[0] + 2):
        lift(u0, 2 * i, 6, e1[3 + i, 7 : 9 + n1[1]])
    coded = code[...]
    start[...] = jnp.where(coded == FREE, delta[...] + whole(u0), coded)
    even = jnp.logical_and(code[rim] == FREE, parity(source_rim.shape, 0) == 0)
    e = start[rim]
    e = jnp.where(
        even,
        (source_rim[...] + flat_of(start, 1, 7, nx + 2, ny + 2) + vertical(e)) * inverse_rim[...],
        e,
    )
    first[rim] = e
    odd = jnp.logical_and(code[own] == FREE, parity((nx, ny, nz), 0) == 1)
    out[...] = jnp.where(odd, odd_half(first), first[own])


def solution(mesh):
    gx, gy = mesh.shape["gx"], mesh.shape["gy"]
    win_x, win_y = min(gx, 2 * REACH + 1), min(gy, 2 * REACH + 1)
    many_x = win_x if win_x == gx else 2 * win_x - 1
    many_y = win_y if win_y == gy else 2 * win_y - 1

    def body(potential, charge, region, volts):
        nx, ny, nz = potential.shape
        f32 = jnp.float32

        def room(x, y, kind=f32):
            return pltpu.VMEM((x, y, nz), kind)

        def halves(x, y):
            return pltpu.VMEM((nz // 128, x, y, 128), f32)

        rows3 = -(-(2 * win_y + 16) // 8) * 8
        scratch = [
            *([room(nx + 4, ny + 16)] * 6),
            *([room(nx + 2, ny + 2)] * 2),
            room(nx, ny, jnp.int32),
            *([room(nx // 2 + 8, ny // 2 + 16)] * 2),
            *([room(nx // 4 + 10, ny // 4 + 12)] * 2),
            pltpu.VMEM((win_x, win_y, nx // 8, ny // 8, nz), f32),
            pltpu.VMEM((win_x, win_y, nx // 8, ny // 8, nz), f32),
            room(2 * win_x, rows3),
            room(2 * win_x, rows3),
            room(2 * win_x + 4, rows3),
            halves(nx // 4 + 10, ny // 4 + 12),
            halves(nx // 2 + 8, ny // 2 + 16),
            halves(nx + 4, ny + 16),
            halves(nx // 2, ny // 2 + 16),
            halves(nx // 4, ny // 4 + 12),
            pltpu.SemaphoreType.DMA((96,)),
            pltpu.SemaphoreType.DMA((96,)),
            pltpu.SemaphoreType.DMA((many_x, many_y)),
            pltpu.SemaphoreType.DMA((win_x, win_y)),
            pltpu.SemaphoreType.DMA((many_x, many_y)),
            pltpu.SemaphoreType.DMA((win_x, win_y)),
            pltpu.SMEM(volts.shape, f32),
            pltpu.SemaphoreType.DMA((4,)),
        ]
        return pl.pallas_call(
            functools.partial(kernel, gx, gy, win_x, win_y),
            out_shape=jax.ShapeDtypeStruct(potential.shape, f32),
            in_specs=[pl.BlockSpec(memory_space=pl.ANY)] * 4,
            out_specs=pl.BlockSpec(memory_space=pltpu.VMEM),
            scratch_shapes=scratch,
            compiler_params=pltpu.CompilerParams(
                collective_id=0, has_side_effects=True, vmem_limit_bytes=60 * 1024 * 1024
            ),
        )(potential, charge, region, volts)

    placed = (P("gx", "gy", None), P("gx", "gy", None), P("gx", "gy", None), P())
    return jax.shard_map(
        body, mesh=mesh, in_specs=placed, out_specs=P("gx", "gy", None), check_vma=False
    )
```

```python
import functools

import jax
import jax.numpy as jnp
from jax import lax
from jax.experimental import pallas as pl
from jax.experimental.pallas import tpu as pltpu
from jax.sharding import PartitionSpec as P

MESH = pl.DeviceIdType.MESH
COARSE_SWEEPS = 4
REACH = 5

FACES = ((1, 0), (-1, 0), (0, 1), (0, -1))
AROUND = FACES + ((1, 1), (1, -1), (-1, 1), (-1, -1))
NEAR = tuple((x, y) for x in range(-2, 3) for y in range(-2, 3) if x or y)
FREE = 1e30


def cut(n, d, low, high):
    first, last = max(0, n * d - low), min(n, n * d + n + high)
    return first, first - n * d, last - first


def kernel(
    gx, gy, win_x, win_y,
    potential, charge, region, volts, out,
    pot, code, chg, delta, source, red_inv, black_inv, ids, inv1, src1, inv2, src2, gat_i, gat_s, inv3, src3, e3, lift2, lift1, u0, u1, u2,
    send_sem, recv_sem, gsend_i, grecv_i, gsend_s, grecv_s, volt, in_sem,
):
    mx, my = lax.axis_index("gx"), lax.axis_index("gy")
    nx, ny, nz = out.shape
    used = [0]

    def here(dx, dy):
        x, y = mx + dx, my + dy
        ok = jnp.bool_(True)
        if dx:
            ok = jnp.logical_and(ok, jnp.logical_and(x >= 0, x < gx))
        if dy:
            ok = jnp.logical_and(ok, jnp.logical_and(y >= 0, y < gy))
        return ok, {"gx": x, "gy": y}

    def exchange(src, src_at, dst, dst_at, n, low, high, offsets):
        copies = []
        for dx, dy in offsets:
            fx, tx, cx = cut(n[0], dx, low, high)
            fy, ty, cy = cut(n[1], dy, low, high)
            ok, target = here(dx, dy)
            copy = pltpu.make_async_remote_copy(
                src_ref=src.at[pl.ds(src_at[0] + fx, cx), pl.ds(src_at[1] + fy, cy), :],
                dst_ref=dst.at[pl.ds(dst_at[0] + tx, cx), pl.ds((dst_at[1] + ty) % dst.shape[1], cy), :],
                send_sem=send_sem.at[used[0]],
                recv_sem=recv_sem.at[used[0]],
                device_id=target,
                device_id_type=MESH,
            )
            used[0] += 1
            pl.when(ok)(copy.start)
            copies.append((ok, here(-dx, -dy)[0], copy))

        def wait():
            for sent, received, copy in copies:
                pl.when(received)(copy.wait_recv)
                pl.when(sent)(copy.wait_send)

        return wait

    def first_of(position, reach, span, total):
        return jnp.clip(position - reach, 0, total - span)

    base_x, base_y = first_of(mx, REACH, win_x, gx), first_of(my, REACH, win_y, gy)
    slot_x, slot_y = mx - base_x, my - base_y
    many_x = win_x if win_x == gx else 2 * win_x - 1
    many_y = win_y if win_y == gy else 2 * win_y - 1

    def partners(act):
        def one(index, carry):
            ix, iy = index // many_y, index % many_y
            tx = ix if win_x == gx else mx + ix - (win_x - 1)
            ty = iy if win_y == gy else my + iy - (win_y - 1)
            sends = (tx != mx) | (ty != my)
            takes = sends
            near_x, near_y, there_x, there_y = tx - base_x, ty - base_y, slot_x, slot_y
            if win_x != gx:
                there_x = mx - first_of(tx, REACH, win_x, gx)
                inside = (tx >= 0) & (tx < gx)
                sends = sends & inside & (there_x >= 0) & (there_x < win_x)
                takes = takes & inside & (near_x >= 0) & (near_x < win_x)
            if win_y != gy:
                there_y = my - first_of(ty, REACH, win_y, gy)
                inside = (ty >= 0) & (ty < gy)
                sends = sends & inside & (there_y >= 0) & (there_y < win_y)
                takes = takes & inside & (near_y >= 0) & (near_y < win_y)
            act((ix, iy), {"gx": tx, "gy": ty}, (near_x, near_y), (there_x, there_y), sends, takes)
            return carry + jnp.where(sends | takes, 1, 0)

        if many_x * many_y > 64:
            return lax.fori_loop(0, many_x * many_y, one, jnp.int32(0))
        for index in range(many_x * many_y):
            one(index, 0)
        return None

    def gather_copy(buffer, ssem, rsem, index, target, slot):
        return pltpu.make_async_remote_copy(
            src_ref=buffer.at[slot_x, slot_y],
            dst_ref=buffer.at[slot[0], slot[1]],
            send_sem=ssem.at[index[0], index[1]],
            recv_sem=rsem.at[slot[0], slot[1]],
            device_id=target,
            device_id_type=MESH,
        )

    def gather_start(buffer, ssem, rsem):
        def act(index, target, near, there, sends, takes):
            pl.when(sends)(gather_copy(buffer, ssem, rsem, index, target, there).start)

        partners(act)

    def gather_wait(buffer, ssem, rsem):
        def act(index, target, near, there, sends, takes):
            pl.when(takes)(gather_copy(buffer, ssem, rsem, index, target, near).wait_recv)
            pl.when(sends)(gather_copy(buffer, ssem, rsem, index, target, there).wait_send)

        partners(act)

    def parity(shape, offset):
        axes = [lax.broadcasted_iota(jnp.int32, shape, d) for d in range(3)]
        return (axes[0] + axes[1] + axes[2] + offset) & 1

    def vertical(v):
        parts = [v[..., 128 * h : 128 * h + 128] for h in range(nz // 128)]
        lane = lax.broadcasted_iota(jnp.int32, parts[0].shape, 2)
        zero = jnp.zeros_like(parts[0])
        ups = [pltpu.roll(part, 127, 2) for part in parts] + [zero]
        downs = [zero] + [pltpu.roll(part, 1, 2) for part in parts]
        return jnp.concatenate(
            [
                jnp.where(lane == 127, ups[h + 1], ups[h]) + jnp.where(lane == 0, downs[h], downs[h + 1])
                for h in range(len(parts))
            ],
            axis=-1,
        )

    def around(v, weight, walled=False):
        rows = v.shape[1]
        zero = jnp.zeros_like(v[:1])
        above, below = pltpu.roll(v, rows - 1, 1), pltpu.roll(v, 1, 1)
        if walled:
            row = lax.broadcasted_iota(jnp.int32, v.shape, 1)
            above = jnp.where(row == rows - 1, 0.0, above)
            below = jnp.where(row == 0, 0.0, below)
        flat = (
            jnp.concatenate([v[1:], zero], axis=0)
            + jnp.concatenate([zero, v[:-1]], axis=0)
            + above
            + below
        )
        return weight * flat + vertical(v)

    lanes = [(h, slice(128 * h, 128 * h + 128)) for h in range(nz // 128)]

    def put(buffer, i, rows, row):
        for h, lane in lanes:
            buffer[h, pl.ds(i, 1), rows] = row[None, :, lane]

    def every_other(buffer, count, y, rows):
        return jnp.concatenate(
            [buffer[h, :count, pl.ds(y, rows, stride=2)] for h, _ in lanes], axis=-1
        )

    def whole(buffer):
        return jnp.concatenate([buffer[h] for h, _ in lanes], axis=-1)

    def lift(buffer, i, low, high):
        for twice in range(2):
            for y in range(2):
                for rows, first in ((low, buffer.shape[2] - 2 * low.shape[0]), (high, 0)):
                    if rows.shape[0] == 1:
                        put(buffer, i + twice, pl.ds(first + y, 1), rows)
                    else:
                        put(buffer, i + twice, pl.ds(first + y, rows.shape[0], stride=2), rows)

    for ref in (pot, chg):
        ref[...] = jnp.zeros(ref.shape, jnp.float32)
    own = (slice(2, nx + 2), slice(0, ny))
    loads = [
        pltpu.make_async_copy(origin, target, in_sem.at[index])
        for index, (origin, target) in enumerate(
            (
                (volts, volt),
                (region, ids),
                (potential, pot.at[own[0], own[1]]),
                (charge, chg.at[own[0], own[1]]),
            )
        )
    ]
    for load in loads:
        load.start()
    for ref in (code, delta, inv1, src1, inv2, src2, inv3, src3, e3, lift1, lift2):
        ref[...] = jnp.zeros(ref.shape, ref.dtype)

    barrier = pltpu.get_barrier_semaphore()

    def greet(index, target, near, there, sends, takes):
        @pl.when(sends | takes)
        def _():
            pl.semaphore_signal(barrier, inc=1, device_id=target, device_id_type=MESH)

    peers = partners(greet)
    if win_x == gx and win_y == gy:
        peers = gx * gy - 1

    for load in loads:
        load.wait()
    coded = jnp.full((nx, ny, nz), FREE, jnp.float32)
    for electrode in range(volts.shape[0]):
        coded = jnp.where(ids[...] == electrode + 1, volt[electrode], coded)
    code[own] = coded

    pl.semaphore_wait(barrier, peers)

    full = (nx, ny)
    wait_code = exchange(code, (2, 0), code, (2, 0), full, 2, 2, AROUND)
    wait_pot = exchange(pot, (2, 0), pot, (2, 0), full, 2, 2, AROUND)
    wait_chg = exchange(chg, (2, 0), chg, (2, 0), full, 1, 1, AROUND)

    bend = 0.5 * jnp.exp(pot[own])

    def coarsened(values, buffer):
        half_x, rows = values.shape[0] // 2, values.shape[1] // 2
        for i in range(half_x):
            put(buffer, i, slice(0, 2 * rows), 0.5 * (values[2 * i] + values[2 * i + 1]))
        return 0.5 * (every_other(buffer, half_x, 0, rows) + every_other(buffer, half_x, 1, rows))

    n1, n2, n3 = (nx // 2, ny // 2), (nx // 4, ny // 4), (nx // 8, ny // 8)
    c1 = coarsened(bend, u0)
    inv1[4 : 4 + n1[0], : n1[1]] = 1.0 / (3.0 + c1)
    c2 = coarsened(c1, u1)
    inv2[5 : 5 + n2[0], : n2[1]] = 1.0 / (2.25 + c2)
    c3 = coarsened(c2, u2)
    gat_i[pl.ds(slot_x, 1), pl.ds(slot_y, 1)] = (1.0 / (2.0625 + c3))[None, None]

    wait_code()
    wait_pot()
    wait_chg()
    wait_inv1 = exchange(inv1, (4, 0), inv1, (4, 0), n1, 4, 4, AROUND)
    wait_inv2 = exchange(inv2, (5, 0), inv2, (5, 0), n2, 5, 5, NEAR)
    gather_start(gat_i, gsend_i, grecv_i)

    def split(inverse, offset, live=None):
        if live is not None:
            inverse = jnp.where(live, inverse, 0.0)
        color = parity(inverse.shape, offset)
        return jnp.where(color == 0, inverse, 0.0), jnp.where(color == 0, 0.0, inverse)

    p, coded = pot[...], code[...]
    free = coded == FREE
    bend = 0.5 * jnp.exp(p)
    red_inv[...], black_inv[...] = split(1.0 / (6.0 + bend), 0, free)
    source[...] = (
        chg[...] - 6.0 * p + around(p + jnp.where(free, 0.0, coded), 1.0) - (bend - 0.5)
    )
    red = source[...] * red_inv[...]
    mid = slice(2, nx + 2)
    rows = slice(0, ny)
    delta[own] = ((source[...] + around(red, 1.0)) * black_inv[...])[mid, rows]
    wait_delta = exchange(delta, (2, 0), delta, (2, 0), full, 2, 2, AROUND)
    wait_inv1()
    wait_inv2()
    wait_delta()

    def narrowed(r, x, count, rows, buffer):
        width = r.shape[1]
        for i in range(count):
            a = x + 2 * i
            plane = 0.25 * r[a : a + 1] + 0.5 * r[a + 1 : a + 2] + 0.25 * r[a + 2 : a + 3]
            put(buffer, i, slice(0, width), pltpu.roll(plane, 1, 1)[0])
        return (
            0.25 * every_other(buffer, count, 0, rows)
            + 0.5 * every_other(buffer, count, 1, rows)
            + 0.25 * every_other(buffer, count, 2, rows)
        )

    r = jnp.where(red_inv[...] > 0.0, around(delta[...], 1.0), 0.0)
    src1[4 : 4 + n1[0], : n1[1]] = narrowed(r, 1, n1[0], n1[1], u0)
    wait_src1 = exchange(src1, (4, 0), src1, (4, 0), n1, 4, 4, AROUND)
    inverses1 = split(inv1[...], 0)
    wait_src1()

    def down(source, inverses, weight):
        red = source * inverses[0]
        black = (source + around(red, weight)) * inverses[1]
        return black, jnp.where(inverses[0] > 0.0, around(black, weight), 0.0)

    def up(black, source, inverses, weight):
        red = (source + around(black, weight)) * inverses[0]
        return red + (source + around(red, weight)) * inverses[1]

    black1, r = down(src1[...], inverses1, 0.25)
    src2[5 : 5 + n2[0], : n2[1]] = narrowed(r, 3, n2[0], n2[1], u1)
    wait_src2 = exchange(src2, (5, 0), src2, (5, 0), n2, 5, 5, NEAR)
    inverses2 = split(inv2[...], 1)
    gather_wait(gat_i, gsend_i, grecv_i)
    for ix in range(win_x):
        for iy in range(win_y):
            inv3[2 * ix : 2 * ix + 2, 2 * iy : 2 * iy + 2] = gat_i[ix, iy]
    inverses3 = split(inv3[...], 0)
    wait_src2()
    black2, r = down(src2[...], inverses2, 0.0625)
    gat_s[pl.ds(slot_x, 1), pl.ds(slot_y, 1)] = narrowed(r, 4, n3[0], n3[1], u2)[None, None]
    gather_start(gat_s, gsend_s, grecv_s)
    gather_wait(gat_s, gsend_s, grecv_s)
    for ix in range(win_x):
        for iy in range(win_y):
            src3[2 * ix : 2 * ix + 2, 2 * iy : 2 * iy + 2] = gat_s[ix, iy]

    def renewed(other, inverse):
        return (src3[...] + around(other, 0.015625, walled=True)) * inverse

    red = src3[...] * inverses3[0]
    for _ in range(COARSE_SWEEPS - 1):
        red = renewed(renewed(red, inverses3[1]), inverses3[0])
    e3[2 : 2 + 2 * win_x, 8 : 8 + src3.shape[1]] = red + renewed(red, inverses3[1])

    for i in range(n3[0] + 4):
        row = e3[pl.ds(2 * slot_x + i, 1)]
        row = pltpu.roll(row, e3.shape[1] - 2 * slot_y, 1)[0]
        lift(lift2, 1 + 2 * i, row[6:8], row[8 : 10 + n3[1]])
    e2 = up(
        black2 + whole(lift2), src2[...], inverses2, 0.0625
    )
    for i in range(n2[0] + 4):
        lift(lift1, 2 * i, e2[3 + i, -2:], e2[3 + i, : 2 + n2[1]])
    e1 = up(black1 + whole(lift1), src1[...], inverses1, 0.25)
    for i in range(n1[0] + 2):
        lift(u0, 2 * i, e1[3 + i, -1:], e1[3 + i, : 1 + n1[1]])
    coded = code[...]
    black = jnp.where(coded == FREE, delta[...] + whole(u0), 0.0)
    e = up(black, source[...], (red_inv[...], black_inv[...]), 1.0)
    out[...] = e[mid, rows] + jnp.where(coded == FREE, 0.0, coded)[mid, rows]


def solution(mesh):
    gx, gy = mesh.shape["gx"], mesh.shape["gy"]
    win_x, win_y = min(gx, 2 * REACH + 1), min(gy, 2 * REACH + 1)
    many_x = win_x if win_x == gx else 2 * win_x - 1
    many_y = win_y if win_y == gy else 2 * win_y - 1

    def body(potential, charge, region, volts):
        nx, ny, nz = potential.shape
        f32 = jnp.float32

        def room(x, y, kind=f32):
            return pltpu.VMEM((x, y, nz), kind)

        def halves(x, y):
            return pltpu.VMEM((nz // 128, x, y, 128), f32)

        rows3 = -(-2 * win_y // 8) * 8
        scratch = [
            *([room(nx + 4, ny + 8)] * 7),
            room(nx, ny, jnp.int32),
            *([room(nx // 2 + 8, ny // 2 + 8)] * 2),
            *([room(nx // 4 + 10, ny // 4 + 12)] * 2),
            pltpu.VMEM((win_x, win_y, nx // 8, ny // 8, nz), f32),
            pltpu.VMEM((win_x, win_y, nx // 8, ny // 8, nz), f32),
            room(2 * win_x, rows3),
            room(2 * win_x, rows3),
            room(2 * win_x + 4, rows3 + 16),
            halves(nx // 4 + 10, ny // 4 + 12),
            halves(nx // 2 + 8, ny // 2 + 8),
            halves(nx + 4, ny + 8),
            halves(nx // 2, ny // 2 + 16),
            halves(nx // 4, ny // 4 + 12),
            pltpu.SemaphoreType.DMA((96,)),
            pltpu.SemaphoreType.DMA((96,)),
            pltpu.SemaphoreType.DMA((many_x, many_y)),
            pltpu.SemaphoreType.DMA((win_x, win_y)),
            pltpu.SemaphoreType.DMA((many_x, many_y)),
            pltpu.SemaphoreType.DMA((win_x, win_y)),
            pltpu.SMEM(volts.shape, f32),
            pltpu.SemaphoreType.DMA((4,)),
        ]
        return pl.pallas_call(
            functools.partial(kernel, gx, gy, win_x, win_y),
            out_shape=jax.ShapeDtypeStruct(potential.shape, f32),
            in_specs=[pl.BlockSpec(memory_space=pl.ANY)] * 4,
            out_specs=pl.BlockSpec(memory_space=pltpu.VMEM),
            scratch_shapes=scratch,
            compiler_params=pltpu.CompilerParams(
                collective_id=0, has_side_effects=True, vmem_limit_bytes=60 * 1024 * 1024
            ),
        )(potential, charge, region, volts)

    placed = (P("gx", "gy", None), P("gx", "gy", None), P("gx", "gy", None), P())
    return jax.shard_map(
        body, mesh=mesh, in_specs=placed, out_specs=P("gx", "gy", None), check_vma=False
    )
```

```python
import functools

import jax
import jax.numpy as jnp
from jax import lax
from jax.experimental import pallas as pl
from jax.experimental.pallas import tpu as pltpu
from jax.sharding import PartitionSpec as P

MESH = pl.DeviceIdType.MESH
COARSE_SWEEPS = 4
REACH = 5

FACES = ((1, 0), (-1, 0), (0, 1), (0, -1))
AROUND = FACES + ((1, 1), (1, -1), (-1, 1), (-1, -1))
NEAR = tuple((x, y) for x in range(-2, 3) for y in range(-2, 3) if x or y)
FREE = 1e30


def cut(n, d, low, high):
    first, last = max(0, n * d - low), min(n, n * d + n + high)
    return first, first - n * d, last - first


def kernel(
    gx, gy, win_x, win_y,
    potential, charge, region, volts, out,
    pot, code, chg, delta, source, red_inv, black_inv, ids, inv1, src1, inv2, src2, gat_i, gat_s, inv3, src3, e3, lift2, lift1, u0, u1, u2,
    send_sem, recv_sem, gsend_i, grecv_i, gsend_s, grecv_s, volt, in_sem,
):
    mx, my = lax.axis_index("gx"), lax.axis_index("gy")
    nx, ny, nz = out.shape
    used = [0]

    def here(dx, dy):
        x, y = mx + dx, my + dy
        ok = jnp.bool_(True)
        if dx:
            ok = jnp.logical_and(ok, jnp.logical_and(x >= 0, x < gx))
        if dy:
            ok = jnp.logical_and(ok, jnp.logical_and(y >= 0, y < gy))
        return ok, {"gx": x, "gy": y}

    def exchange(src, src_at, dst, dst_at, n, low, high, offsets):
        copies = []
        for dx, dy in offsets:
            fx, tx, cx = cut(n[0], dx, low, high)
            fy, ty, cy = cut(n[1], dy, low, high)
            ok, target = here(dx, dy)
            copy = pltpu.make_async_remote_copy(
                src_ref=src.at[pl.ds(src_at[0] + fx, cx), pl.ds(src_at[1] + fy, cy), :],
                dst_ref=dst.at[pl.ds(dst_at[0] + tx, cx), pl.ds((dst_at[1] + ty) % dst.shape[1], cy), :],
                send_sem=send_sem.at[used[0]],
                recv_sem=recv_sem.at[used[0]],
                device_id=target,
                device_id_type=MESH,
            )
            used[0] += 1
            pl.when(ok)(copy.start)
            copies.append((ok, here(-dx, -dy)[0], copy))

        def wait():
            for sent, received, copy in copies:
                pl.when(received)(copy.wait_recv)
                pl.when(sent)(copy.wait_send)

        return wait

    def first_of(position, reach, span, total):
        return jnp.clip(position - reach, 0, total - span)

    base_x, base_y = first_of(mx, REACH, win_x, gx), first_of(my, REACH, win_y, gy)
    slot_x, slot_y = mx - base_x, my - base_y
    many_x = win_x if win_x == gx else 2 * win_x - 1
    many_y = win_y if win_y == gy else 2 * win_y - 1

    def partners(act):
        def one(index, carry):
            ix, iy = index // many_y, index % many_y
            tx = ix if win_x == gx else mx + ix - (win_x - 1)
            ty = iy if win_y == gy else my + iy - (win_y - 1)
            sends = (tx != mx) | (ty != my)
            takes = sends
            near_x, near_y, there_x, there_y = tx - base_x, ty - base_y, slot_x, slot_y
            if win_x != gx:
                there_x = mx - first_of(tx, REACH, win_x, gx)
                inside = (tx >= 0) & (tx < gx)
                sends = sends & inside & (there_x >= 0) & (there_x < win_x)
                takes = takes & inside & (near_x >= 0) & (near_x < win_x)
            if win_y != gy:
                there_y = my - first_of(ty, REACH, win_y, gy)
                inside = (ty >= 0) & (ty < gy)
                sends = sends & inside & (there_y >= 0) & (there_y < win_y)
                takes = takes & inside & (near_y >= 0) & (near_y < win_y)
            act((ix, iy), {"gx": tx, "gy": ty}, (near_x, near_y), (there_x, there_y), sends, takes)
            return carry + jnp.where(sends | takes, 1, 0)

        if many_x * many_y > 64:
            return lax.fori_loop(0, many_x * many_y, one, jnp.int32(0))
        for index in range(many_x * many_y):
            one(index, 0)
        return None

    def gather_copy(buffer, ssem, rsem, index, target, slot):
        return pltpu.make_async_remote_copy(
            src_ref=buffer.at[slot_x, slot_y],
            dst_ref=buffer.at[slot[0], slot[1]],
            send_sem=ssem.at[index[0], index[1]],
            recv_sem=rsem.at[slot[0], slot[1]],
            device_id=target,
            device_id_type=MESH,
        )

    def gather_start(buffer, ssem, rsem):
        def act(index, target, near, there, sends, takes):
            pl.when(sends)(gather_copy(buffer, ssem, rsem, index, target, there).start)

        partners(act)

    def gather_wait(buffer, ssem, rsem):
        def act(index, target, near, there, sends, takes):
            pl.when(takes)(gather_copy(buffer, ssem, rsem, index, target, near).wait_recv)
            pl.when(sends)(gather_copy(buffer, ssem, rsem, index, target, there).wait_send)

        partners(act)

    def parity(shape, offset):
        axes = [lax.broadcasted_iota(jnp.int32, shape, d) for d in range(3)]
        return (axes[0] + axes[1] + axes[2] + offset) & 1

    def vertical(v):
        parts = [v[..., 128 * h : 128 * h + 128] for h in range(nz // 128)]
        lane = lax.broadcasted_iota(jnp.int32, parts[0].shape, 2)
        zero = jnp.zeros_like(parts[0])
        ups = [pltpu.roll(part, 127, 2) for part in parts] + [zero]
        downs = [zero] + [pltpu.roll(part, 1, 2) for part in parts]
        return jnp.concatenate(
            [
                jnp.where(lane == 127, ups[h + 1], ups[h]) + jnp.where(lane == 0, downs[h], downs[h + 1])
                for h in range(len(parts))
            ],
            axis=-1,
        )

    def around(v, weight, walled=False):
        rows = v.shape[1]
        zero = jnp.zeros_like(v[:1])
        above, below = pltpu.roll(v, rows - 1, 1), pltpu.roll(v, 1, 1)
        if walled:
            row = lax.broadcasted_iota(jnp.int32, v.shape, 1)
            above = jnp.where(row == rows - 1, 0.0, above)
            below = jnp.where(row == 0, 0.0, below)
        flat = (
            jnp.concatenate([v[1:], zero], axis=0)
            + jnp.concatenate([zero, v[:-1]], axis=0)
            + above
            + below
        )
        return weight * flat + vertical(v)

    lanes = [(h, slice(128 * h, 128 * h + 128)) for h in range(nz // 128)]

    def put(buffer, i, rows, row):
        for h, lane in lanes:
            buffer[h, pl.ds(i, 1), rows] = row[None, :, lane]

    def every_other(buffer, count, y, rows):
        return jnp.concatenate(
            [buffer[h, :count, pl.ds(y, rows, stride=2)] for h, _ in lanes], axis=-1
        )

    def whole(buffer):
        return jnp.concatenate([buffer[h] for h, _ in lanes], axis=-1)

    def lift(buffer, i, low, high):
        for twice in range(2):
            for y in range(2):
                for rows, first in ((low, buffer.shape[2] - 2 * low.shape[0]), (high, 0)):
                    if rows.shape[0] == 1:
                        put(buffer, i + twice, pl.ds(first + y, 1), rows)
                    else:
                        put(buffer, i + twice, pl.ds(first + y, rows.shape[0], stride=2), rows)

    for ref in (pot, chg):
        ref[...] = jnp.zeros(ref.shape, jnp.float32)
    own = (slice(2, nx + 2), slice(0, ny))
    loads = [
        pltpu.make_async_copy(origin, target, in_sem.at[index])
        for index, (origin, target) in enumerate(
            (
                (volts, volt),
                (region, ids),
                (potential, pot.at[own[0], own[1]]),
                (charge, chg.at[own[0], own[1]]),
            )
        )
    ]
    for load in loads:
        load.start()
    for ref in (code, delta, inv1, src1, inv2, src2, inv3, src3, e3, lift1, lift2):
        ref[...] = jnp.zeros(ref.shape, ref.dtype)

    barrier = pltpu.get_barrier_semaphore()

    def greet(index, target, near, there, sends, takes):
        @pl.when(sends | takes)
        def _():
            pl.semaphore_signal(barrier, inc=1, device_id=target, device_id_type=MESH)

    peers = partners(greet)
    if win_x == gx and win_y == gy:
        peers = gx * gy - 1

    for load in loads:
        load.wait()
    coded = jnp.full((nx, ny, nz), FREE, jnp.float32)
    for electrode in range(volts.shape[0]):
        coded = jnp.where(ids[...] == electrode + 1, volt[electrode], coded)
    code[own] = coded

    pl.semaphore_wait(barrier, peers)

    full = (nx, ny)
    wait_code = exchange(code, (2, 0), code, (2, 0), full, 2, 2, AROUND)
    wait_pot = exchange(pot, (2, 0), pot, (2, 0), full, 2, 2, AROUND)
    wait_chg = exchange(chg, (2, 0), chg, (2, 0), full, 1, 1, AROUND)

    bend = 0.5 * jnp.exp(pot[own])

    def coarsened(values, buffer):
        half_x, rows = values.shape[0] // 2, values.shape[1] // 2
        for i in range(half_x):
            put(buffer, i, slice(0, 2 * rows), 0.5 * (values[2 * i] + values[2 * i + 1]))
        return 0.5 * (every_other(buffer, half_x, 0, rows) + every_other(buffer, half_x, 1, rows))

    n1, n2, n3 = (nx // 2, ny // 2), (nx // 4, ny // 4), (nx // 8, ny // 8)
    c1 = coarsened(bend, u0)
    inv1[4 : 4 + n1[0], : n1[1]] = 1.0 / (3.0 + c1)
    c2 = coarsened(c1, u1)
    inv2[5 : 5 + n2[0], : n2[1]] = 1.0 / (2.25 + c2)
    c3 = coarsened(c2, u2)
    gat_i[pl.ds(slot_x, 1), pl.ds(slot_y, 1)] = (1.0 / (2.0625 + c3))[None, None]

    wait_inv1 = exchange(inv1, (4, 0), inv1, (4, 0), n1, 4, 4, AROUND)
    wait_inv2 = exchange(inv2, (5, 0), inv2, (5, 0), n2, 5, 5, NEAR)
    gather_start(gat_i, gsend_i, grecv_i)
    wait_code()
    wait_pot()
    wait_chg()

    def split(inverse, offset, live=None):
        if live is not None:
            inverse = jnp.where(live, inverse, 0.0)
        color = parity(inverse.shape, offset)
        return jnp.where(color == 0, inverse, 0.0), jnp.where(color == 0, 0.0, inverse)

    p, coded = pot[...], code[...]
    free = coded == FREE
    bend = 0.5 * jnp.exp(p)
    red_inv[...], black_inv[...] = split(1.0 / (6.0 + bend), 0, free)
    source[...] = (
        chg[...] - 6.0 * p + around(p + jnp.where(free, 0.0, coded), 1.0) - (bend - 0.5)
    )
    red = source[...] * red_inv[...]
    mid = slice(2, nx + 2)
    rows = slice(0, ny)
    delta[own] = ((source[...] + around(red, 1.0)) * black_inv[...])[mid, rows]
    wait_delta = exchange(delta, (2, 0), delta, (2, 0), full, 2, 2, AROUND)
    wait_delta()

    def narrowed(r, x, count, rows, buffer):
        width = r.shape[1]
        for i in range(count):
            a = x + 2 * i
            plane = 0.25 * r[a : a + 1] + 0.5 * r[a + 1 : a + 2] + 0.25 * r[a + 2 : a + 3]
            put(buffer, i, slice(0, width), pltpu.roll(plane, 1, 1)[0])
        return (
            0.25 * every_other(buffer, count, 0, rows)
            + 0.5 * every_other(buffer, count, 1, rows)
            + 0.25 * every_other(buffer, count, 2, rows)
        )

    r = jnp.where(red_inv[...] > 0.0, around(delta[...], 1.0), 0.0)
    src1[4 : 4 + n1[0], : n1[1]] = narrowed(r, 1, n1[0], n1[1], u0)
    wait_src1 = exchange(src1, (4, 0), src1, (4, 0), n1, 4, 4, AROUND)
    wait_inv1()
    inverses1 = split(inv1[...], 0)
    wait_src1()

    def down(source, inverses, weight):
        red = source * inverses[0]
        black = (source + around(red, weight)) * inverses[1]
        return black, jnp.where(inverses[0] > 0.0, around(black, weight), 0.0)

    def up(black, source, inverses, weight):
        red = (source + around(black, weight)) * inverses[0]
        return red + (source + around(red, weight)) * inverses[1]

    black1, r = down(src1[...], inverses1, 0.25)
    src2[5 : 5 + n2[0], : n2[1]] = narrowed(r, 3, n2[0], n2[1], u1)
    wait_src2 = exchange(src2, (5, 0), src2, (5, 0), n2, 5, 5, NEAR)
    wait_inv2()
    inverses2 = split(inv2[...], 1)
    gather_wait(gat_i, gsend_i, grecv_i)
    for ix in range(win_x):
        for iy in range(win_y):
            inv3[2 * ix : 2 * ix + 2, 2 * iy : 2 * iy + 2] = gat_i[ix, iy]
    inverses3 = split(inv3[...], 0)
    wait_src2()
    black2, r = down(src2[...], inverses2, 0.0625)
    gat_s[pl.ds(slot_x, 1), pl.ds(slot_y, 1)] = narrowed(r, 4, n3[0], n3[1], u2)[None, None]
    gather_start(gat_s, gsend_s, grecv_s)
    gather_wait(gat_s, gsend_s, grecv_s)
    for ix in range(win_x):
        for iy in range(win_y):
            src3[2 * ix : 2 * ix + 2, 2 * iy : 2 * iy + 2] = gat_s[ix, iy]

    def renewed(other, inverse):
        return (src3[...] + around(other, 0.015625, walled=True)) * inverse

    red = src3[...] * inverses3[0]
    for _ in range(COARSE_SWEEPS - 1):
        red = renewed(renewed(red, inverses3[1]), inverses3[0])
    e3[2 : 2 + 2 * win_x, 8 : 8 + src3.shape[1]] = red + renewed(red, inverses3[1])

    for i in range(n3[0] + 4):
        row = e3[pl.ds(2 * slot_x + i, 1)]
        row = pltpu.roll(row, e3.shape[1] - 2 * slot_y, 1)[0]
        lift(lift2, 1 + 2 * i, row[6:8], row[8 : 10 + n3[1]])
    e2 = up(
        black2 + whole(lift2), src2[...], inverses2, 0.0625
    )
    for i in range(n2[0] + 4):
        lift(lift1, 2 * i, e2[3 + i, -2:], e2[3 + i, : 2 + n2[1]])
    e1 = up(black1 + whole(lift1), src1[...], inverses1, 0.25)
    for i in range(n1[0] + 2):
        lift(u0, 2 * i, e1[3 + i, -1:], e1[3 + i, : 1 + n1[1]])
    coded = code[...]
    black = jnp.where(coded == FREE, delta[...] + whole(u0), 0.0)
    e = up(black, source[...], (red_inv[...], black_inv[...]), 1.0)
    out[...] = e[mid, rows] + jnp.where(coded == FREE, 0.0, coded)[mid, rows]


def solution(mesh):
    gx, gy = mesh.shape["gx"], mesh.shape["gy"]
    win_x, win_y = min(gx, 2 * REACH + 1), min(gy, 2 * REACH + 1)
    many_x = win_x if win_x == gx else 2 * win_x - 1
    many_y = win_y if win_y == gy else 2 * win_y - 1

    def body(potential, charge, region, volts):
        nx, ny, nz = potential.shape
        f32 = jnp.float32

        def room(x, y, kind=f32):
            return pltpu.VMEM((x, y, nz), kind)

        def halves(x, y):
            return pltpu.VMEM((nz // 128, x, y, 128), f32)

        rows3 = -(-2 * win_y // 8) * 8
        scratch = [
            *([room(nx + 4, ny + 8)] * 7),
            room(nx, ny, jnp.int32),
            *([room(nx // 2 + 8, ny // 2 + 8)] * 2),
            *([room(nx // 4 + 10, ny // 4 + 12)] * 2),
            pltpu.VMEM((win_x, win_y, nx // 8, ny // 8, nz), f32),
            pltpu.VMEM((win_x, win_y, nx // 8, ny // 8, nz), f32),
            room(2 * win_x, rows3),
            room(2 * win_x, rows3),
            room(2 * win_x + 4, rows3 + 16),
            halves(nx // 4 + 10, ny // 4 + 12),
            halves(nx // 2 + 8, ny // 2 + 8),
            halves(nx + 4, ny + 8),
            halves(nx // 2, ny // 2 + 16),
            halves(nx // 4, ny // 4 + 12),
            pltpu.SemaphoreType.DMA((96,)),
            pltpu.SemaphoreType.DMA((96,)),
            pltpu.SemaphoreType.DMA((many_x, many_y)),
            pltpu.SemaphoreType.DMA((win_x, win_y)),
            pltpu.SemaphoreType.DMA((many_x, many_y)),
            pltpu.SemaphoreType.DMA((win_x, win_y)),
            pltpu.SMEM(volts.shape, f32),
            pltpu.SemaphoreType.DMA((4,)),
        ]
        return pl.pallas_call(
            functools.partial(kernel, gx, gy, win_x, win_y),
            out_shape=jax.ShapeDtypeStruct(potential.shape, f32),
            in_specs=[pl.BlockSpec(memory_space=pltpu.HBM)] * 4,
            out_specs=pl.BlockSpec(memory_space=pltpu.VMEM),
            scratch_shapes=scratch,
            compiler_params=pltpu.CompilerParams(
                collective_id=0, has_side_effects=True, vmem_limit_bytes=32 * 1024 * 1024
            ),
        )(potential, charge, region, volts)

    placed = (P("gx", "gy", None), P("gx", "gy", None), P("gx", "gy", None), P())
    return jax.shard_map(
        body, mesh=mesh, in_specs=placed, out_specs=P("gx", "gy", None), check_vma=False
    )
```

```python
import functools

import jax
import jax.numpy as jnp
from jax import lax
from jax.experimental import pallas as pl
from jax.experimental.pallas import tpu as pltpu
from jax.sharding import PartitionSpec as P

MESH = pl.DeviceIdType.MESH
COARSE_SWEEPS = 4
REACH = 5

FACES = ((0, 1), (0, -1), (1, 0), (-1, 0))
AROUND = FACES + ((1, 1), (1, -1), (-1, 1), (-1, -1))
NEAR = tuple((x, y) for x in range(-2, 3) for y in range(-2, 3) if x or y)
FREE = 1e30


def cut(n, d, low, high):
    first, last = max(0, n * d - low), min(n, n * d + n + high)
    return first, first - n * d, last - first


def kernel(
    gx, gy, win_x, win_y,
    potential, charge, region, volts, out,
    pot, code, chg, delta, source, red_inv, black_inv, ids, inv1, src1, inv2, src2, gat_i, gat_s, inv3, src3, e3, lift2, lift1, u0, u1, u2,
    send_sem, recv_sem, gsend_i, grecv_i, gsend_s, grecv_s, volt, in_sem,
):
    mx, my = lax.axis_index("gx"), lax.axis_index("gy")
    nx, ny, nz = out.shape
    used = [0]

    def here(dx, dy):
        x, y = mx + dx, my + dy
        ok = jnp.bool_(True)
        if dx:
            ok = jnp.logical_and(ok, jnp.logical_and(x >= 0, x < gx))
        if dy:
            ok = jnp.logical_and(ok, jnp.logical_and(y >= 0, y < gy))
        return ok, {"gx": x, "gy": y}

    def exchange(src, src_at, dst, dst_at, n, low, high, offsets):
        copies = []
        for dx, dy in offsets:
            fx, tx, cx = cut(n[0], dx, low, high)
            fy, ty, cy = cut(n[1], dy, low, high)
            ok, target = here(dx, dy)
            copy = pltpu.make_async_remote_copy(
                src_ref=src.at[pl.ds(src_at[0] + fx, cx), pl.ds(src_at[1] + fy, cy), :],
                dst_ref=dst.at[pl.ds(dst_at[0] + tx, cx), pl.ds((dst_at[1] + ty) % dst.shape[1], cy), :],
                send_sem=send_sem.at[used[0]],
                recv_sem=recv_sem.at[used[0]],
                device_id=target,
                device_id_type=MESH,
            )
            used[0] += 1
            pl.when(ok)(copy.start)
            copies.append((ok, here(-dx, -dy)[0], copy))

        def wait():
            for sent, received, copy in copies:
                pl.when(received)(copy.wait_recv)
                pl.when(sent)(copy.wait_send)

        return wait

    def first_of(position, reach, span, total):
        return jnp.clip(position - reach, 0, total - span)

    base_x, base_y = first_of(mx, REACH, win_x, gx), first_of(my, REACH, win_y, gy)
    slot_x, slot_y = mx - base_x, my - base_y
    many_x = win_x if win_x == gx else 2 * win_x - 1
    many_y = win_y if win_y == gy else 2 * win_y - 1

    def partners(act):
        def one(index, carry):
            ix, iy = index // many_y, index % many_y
            tx = ix if win_x == gx else mx + ix - (win_x - 1)
            ty = iy if win_y == gy else my + iy - (win_y - 1)
            sends = (tx != mx) | (ty != my)
            takes = sends
            near_x, near_y, there_x, there_y = tx - base_x, ty - base_y, slot_x, slot_y
            if win_x != gx:
                there_x = mx - first_of(tx, REACH, win_x, gx)
                inside = (tx >= 0) & (tx < gx)
                sends = sends & inside & (there_x >= 0) & (there_x < win_x)
                takes = takes & inside & (near_x >= 0) & (near_x < win_x)
            if win_y != gy:
                there_y = my - first_of(ty, REACH, win_y, gy)
                inside = (ty >= 0) & (ty < gy)
                sends = sends & inside & (there_y >= 0) & (there_y < win_y)
                takes = takes & inside & (near_y >= 0) & (near_y < win_y)
            act((ix, iy), {"gx": tx, "gy": ty}, (near_x, near_y), (there_x, there_y), sends, takes)
            return carry + jnp.where(sends | takes, 1, 0)

        if many_x * many_y > 64:
            return lax.fori_loop(0, many_x * many_y, one, jnp.int32(0))
        for index in range(many_x * many_y):
            one(index, 0)
        return None

    def gather_copy(buffer, ssem, rsem, index, target, slot):
        return pltpu.make_async_remote_copy(
            src_ref=buffer.at[slot_x, slot_y],
            dst_ref=buffer.at[slot[0], slot[1]],
            send_sem=ssem.at[index[0], index[1]],
            recv_sem=rsem.at[slot[0], slot[1]],
            device_id=target,
            device_id_type=MESH,
        )

    def gather_start(buffer, ssem, rsem):
        def act(index, target, near, there, sends, takes):
            pl.when(sends)(gather_copy(buffer, ssem, rsem, index, target, there).start)

        partners(act)

    def gather_wait(buffer, ssem, rsem):
        def act(index, target, near, there, sends, takes):
            pl.when(takes)(gather_copy(buffer, ssem, rsem, index, target, near).wait_recv)
            pl.when(sends)(gather_copy(buffer, ssem, rsem, index, target, there).wait_send)

        partners(act)

    def parity(shape, offset):
        axes = [lax.broadcasted_iota(jnp.int32, shape, d) for d in range(3)]
        return (axes[0] + axes[1] + axes[2] + offset) & 1

    def vertical(v):
        parts = [v[..., 128 * h : 128 * h + 128] for h in range(nz // 128)]
        lane = lax.broadcasted_iota(jnp.int32, parts[0].shape, 2)
        zero = jnp.zeros_like(parts[0])
        ups = [pltpu.roll(part, 127, 2) for part in parts] + [zero]
        downs = [zero] + [pltpu.roll(part, 1, 2) for part in parts]
        return jnp.concatenate(
            [
                jnp.where(lane == 127, ups[h + 1], ups[h]) + jnp.where(lane == 0, downs[h], downs[h + 1])
                for h in range(len(parts))
            ],
            axis=-1,
        )

    def around(v, weight, walled=False):
        rows = v.shape[1]
        zero = jnp.zeros_like(v[:1])
        above, below = pltpu.roll(v, rows - 1, 1), pltpu.roll(v, 1, 1)
        if walled:
            row = lax.broadcasted_iota(jnp.int32, v.shape, 1)
            above = jnp.where(row == rows - 1, 0.0, above)
            below = jnp.where(row == 0, 0.0, below)
        flat = (
            jnp.concatenate([v[1:], zero], axis=0)
            + jnp.concatenate([zero, v[:-1]], axis=0)
            + above
            + below
        )
        return weight * flat + vertical(v)

    lanes = [(h, slice(128 * h, 128 * h + 128)) for h in range(nz // 128)]

    def put(buffer, i, rows, row):
        for h, lane in lanes:
            buffer[h, pl.ds(i, 1), rows] = row[None, :, lane]

    def every_other(buffer, count, y, rows):
        return jnp.concatenate(
            [buffer[h, :count, pl.ds(y, rows, stride=2)] for h, _ in lanes], axis=-1
        )

    def whole(buffer):
        return jnp.concatenate([buffer[h] for h, _ in lanes], axis=-1)

    def lift(buffer, i, low, high):
        for twice in range(2):
            for y in range(2):
                for rows, first in ((low, buffer.shape[2] - 2 * low.shape[0]), (high, 0)):
                    if rows.shape[0] == 1:
                        put(buffer, i + twice, pl.ds(first + y, 1), rows)
                    else:
                        put(buffer, i + twice, pl.ds(first + y, rows.shape[0], stride=2), rows)

    for ref in (pot, chg):
        ref[...] = jnp.zeros(ref.shape, jnp.float32)
    own = (slice(2, nx + 2), slice(0, ny))
    loads = [
        pltpu.make_async_copy(origin, target, in_sem.at[index])
        for index, (origin, target) in enumerate(
            (
                (volts, volt),
                (region, ids),
                (potential, pot.at[own[0], own[1]]),
                (charge, chg.at[own[0], own[1]]),
            )
        )
    ]
    for load in loads:
        load.start()
    for ref in (code, delta, inv1, src1, inv2, src2, inv3, src3, e3, lift1, lift2):
        ref[...] = jnp.zeros(ref.shape, ref.dtype)

    barrier = pltpu.get_barrier_semaphore()

    def greet(index, target, near, there, sends, takes):
        @pl.when(sends | takes)
        def _():
            pl.semaphore_signal(barrier, inc=1, device_id=target, device_id_type=MESH)

    peers = partners(greet)
    if win_x == gx and win_y == gy:
        peers = gx * gy - 1

    for load in loads:
        load.wait()
    coded = jnp.full((nx, ny, nz), FREE, jnp.float32)
    for electrode in range(volts.shape[0]):
        coded = jnp.where(ids[...] == electrode + 1, volt[electrode], coded)
    code[own] = coded

    pl.semaphore_wait(barrier, peers)

    full = (nx, ny)
    wait_code = exchange(code, (2, 0), code, (2, 0), full, 2, 2, AROUND)
    wait_pot = exchange(pot, (2, 0), pot, (2, 0), full, 2, 2, AROUND)
    wait_chg = exchange(chg, (2, 0), chg, (2, 0), full, 1, 1, AROUND)

    bend = 0.5 * jnp.exp(pot[own])

    def coarsened(values, buffer):
        half_x, rows = values.shape[0] // 2, values.shape[1] // 2
        for i in range(half_x):
            put(buffer, i, slice(0, 2 * rows), 0.5 * (values[2 * i] + values[2 * i + 1]))
        return 0.5 * (every_other(buffer, half_x, 0, rows) + every_other(buffer, half_x, 1, rows))

    n1, n2, n3 = (nx // 2, ny // 2), (nx // 4, ny // 4), (nx // 8, ny // 8)
    c1 = coarsened(bend, u0)
    inv1[4 : 4 + n1[0], : n1[1]] = 1.0 / (3.0 + c1)
    c2 = coarsened(c1, u1)
    inv2[5 : 5 + n2[0], : n2[1]] = 1.0 / (2.25 + c2)
    c3 = coarsened(c2, u2)
    gat_i[pl.ds(slot_x, 1), pl.ds(slot_y, 1)] = (1.0 / (2.0625 + c3))[None, None]

    wait_inv1 = exchange(inv1, (4, 0), inv1, (4, 0), n1, 4, 4, AROUND)
    wait_inv2 = exchange(inv2, (5, 0), inv2, (5, 0), n2, 5, 5, NEAR)
    gather_start(gat_i, gsend_i, grecv_i)
    wait_code()
    wait_pot()
    wait_chg()

    def split(inverse, offset, live=None):
        if live is not None:
            inverse = jnp.where(live, inverse, 0.0)
        color = parity(inverse.shape, offset)
        return jnp.where(color == 0, inverse, 0.0), jnp.where(color == 0, 0.0, inverse)

    p, coded = pot[...], code[...]
    free = coded == FREE
    bend = 0.5 * jnp.exp(p)
    red_inv[...], black_inv[...] = split(1.0 / (6.0 + bend), 0, free)
    source[...] = (
        chg[...] - 6.0 * p + around(p + jnp.where(free, 0.0, coded), 1.0) - (bend - 0.5)
    )
    red = source[...] * red_inv[...]
    mid = slice(2, nx + 2)
    rows = slice(0, ny)
    delta[own] = ((source[...] + around(red, 1.0)) * black_inv[...])[mid, rows]
    wait_delta = exchange(delta, (2, 0), delta, (2, 0), full, 2, 2, AROUND)
    wait_delta()

    def narrowed(r, x, count, rows, buffer):
        width = r.shape[1]
        for i in range(count):
            a = x + 2 * i
            plane = 0.25 * r[a : a + 1] + 0.5 * r[a + 1 : a + 2] + 0.25 * r[a + 2 : a + 3]
            put(buffer, i, slice(0, width), pltpu.roll(plane, 1, 1)[0])
        return (
            0.25 * every_other(buffer, count, 0, rows)
            + 0.5 * every_other(buffer, count, 1, rows)
            + 0.25 * every_other(buffer, count, 2, rows)
        )

    r = jnp.where(red_inv[...] > 0.0, around(delta[...], 1.0), 0.0)
    src1[4 : 4 + n1[0], : n1[1]] = narrowed(r, 1, n1[0], n1[1], u0)
    wait_src1 = exchange(src1, (4, 0), src1, (4, 0), n1, 4, 4, AROUND)
    wait_inv1()
    inverses1 = split(inv1[...], 0)
    wait_src1()

    def down(source, inverses, weight):
        red = source * inverses[0]
        black = (source + around(red, weight)) * inverses[1]
        return black, jnp.where(inverses[0] > 0.0, around(black, weight), 0.0)

    def up(black, source, inverses, weight):
        red = (source + around(black, weight)) * inverses[0]
        return red + (source + around(red, weight)) * inverses[1]

    black1, r = down(src1[...], inverses1, 0.25)
    src2[5 : 5 + n2[0], : n2[1]] = narrowed(r, 3, n2[0], n2[1], u1)
    wait_src2 = exchange(src2, (5, 0), src2, (5, 0), n2, 5, 5, NEAR)
    wait_inv2()
    inverses2 = split(inv2[...], 1)
    gather_wait(gat_i, gsend_i, grecv_i)
    for ix in range(win_x):
        for iy in range(win_y):
            inv3[2 * ix : 2 * ix + 2, 2 * iy : 2 * iy + 2] = gat_i[ix, iy]
    inverses3 = split(inv3[...], 0)
    wait_src2()
    black2, r = down(src2[...], inverses2, 0.0625)
    gat_s[pl.ds(slot_x, 1), pl.ds(slot_y, 1)] = narrowed(r, 4, n3[0], n3[1], u2)[None, None]
    gather_start(gat_s, gsend_s, grecv_s)
    gather_wait(gat_s, gsend_s, grecv_s)
    for ix in range(win_x):
        for iy in range(win_y):
            src3[2 * ix : 2 * ix + 2, 2 * iy : 2 * iy + 2] = gat_s[ix, iy]

    def renewed(other, inverse):
        return (src3[...] + around(other, 0.015625, walled=True)) * inverse

    red = src3[...] * inverses3[0]
    for _ in range(COARSE_SWEEPS - 1):
        red = renewed(renewed(red, inverses3[1]), inverses3[0])
    e3[2 : 2 + 2 * win_x, 8 : 8 + src3.shape[1]] = red + renewed(red, inverses3[1])

    for i in range(n3[0] + 4):
        row = e3[pl.ds(2 * slot_x + i, 1)]
        row = pltpu.roll(row, e3.shape[1] - 2 * slot_y, 1)[0]
        lift(lift2, 1 + 2 * i, row[6:8], row[8 : 10 + n3[1]])
    e2 = up(
        black2 + whole(lift2), src2[...], inverses2, 0.0625
    )
    for i in range(n2[0] + 4):
        lift(lift1, 2 * i, e2[3 + i, -2:], e2[3 + i, : 2 + n2[1]])
    e1 = up(black1 + whole(lift1), src1[...], inverses1, 0.25)
    for i in range(n1[0] + 2):
        lift(u0, 2 * i, e1[3 + i, -1:], e1[3 + i, : 1 + n1[1]])
    coded = code[...]
    black = jnp.where(coded == FREE, delta[...] + whole(u0), 0.0)
    e = up(black, source[...], (red_inv[...], black_inv[...]), 1.0)
    out[...] = e[mid, rows] + jnp.where(coded == FREE, 0.0, coded)[mid, rows]


def solution(mesh):
    gx, gy = mesh.shape["gx"], mesh.shape["gy"]
    win_x, win_y = min(gx, 2 * REACH + 1), min(gy, 2 * REACH + 1)
    many_x = win_x if win_x == gx else 2 * win_x - 1
    many_y = win_y if win_y == gy else 2 * win_y - 1

    def body(potential, charge, region, volts):
        nx, ny, nz = potential.shape
        f32 = jnp.float32

        def room(x, y, kind=f32):
            return pltpu.VMEM((x, y, nz), kind)

        def halves(x, y):
            return pltpu.VMEM((nz // 128, x, y, 128), f32)

        rows3 = -(-2 * win_y // 8) * 8
        scratch = [
            *([room(nx + 4, ny + 8)] * 7),
            room(nx, ny, jnp.int32),
            *([room(nx // 2 + 8, ny // 2 + 8)] * 2),
            *([room(nx // 4 + 10, ny // 4 + 12)] * 2),
            pltpu.VMEM((win_x, win_y, nx // 8, ny // 8, nz), f32),
            pltpu.VMEM((win_x, win_y, nx // 8, ny // 8, nz), f32),
            room(2 * win_x, rows3),
            room(2 * win_x, rows3),
            room(2 * win_x + 4, rows3 + 16),
            halves(nx // 4 + 10, ny // 4 + 12),
            halves(nx // 2 + 8, ny // 2 + 8),
            halves(nx + 4, ny + 8),
            halves(nx // 2, ny // 2 + 16),
            halves(nx // 4, ny // 4 + 12),
            pltpu.SemaphoreType.DMA((96,)),
            pltpu.SemaphoreType.DMA((96,)),
            pltpu.SemaphoreType.DMA((many_x, many_y)),
            pltpu.SemaphoreType.DMA((win_x, win_y)),
            pltpu.SemaphoreType.DMA((many_x, many_y)),
            pltpu.SemaphoreType.DMA((win_x, win_y)),
            pltpu.SMEM(volts.shape, f32),
            pltpu.SemaphoreType.DMA((4,)),
        ]
        return pl.pallas_call(
            functools.partial(kernel, gx, gy, win_x, win_y),
            out_shape=jax.ShapeDtypeStruct(potential.shape, f32),
            in_specs=[pl.BlockSpec(memory_space=pl.ANY)] * 4,
            out_specs=pl.BlockSpec(memory_space=pltpu.VMEM),
            scratch_shapes=scratch,
            compiler_params=pltpu.CompilerParams(
                collective_id=0, has_side_effects=True, vmem_limit_bytes=60 * 1024 * 1024
            ),
        )(potential, charge, region, volts)

    placed = (P("gx", "gy", None), P("gx", "gy", None), P("gx", "gy", None), P())
    return jax.shard_map(
        body, mesh=mesh, in_specs=placed, out_specs=P("gx", "gy", None), check_vma=False
    )
```
